512 devices in a mesh: replica: 4 (over x), fsdp: 128 (over y, z, core).
Axes of the slice: x: 4, y: 4, z: 16, core: 2. Of those that a mesh axis runs over, the one named last changes fastest.
Arguments:
- pseudo_grads: bfloat16 [4, 6144, 16384], P('replica', 'fsdp')
- outer_params: float32 [6144, 16384], P('replica', 'fsdp'), may hold values from -6 to 6
- momentum: float32 [6144, 16384], P('replica', 'fsdp'), may hold values from -0.6 to 0.6
- clip_level: float32 [1], replicated, may hold values from 0.05 to 0.2
- block_picks: int32 [4, 128, 4, 6], P(None, 'fsdp'), may hold values from -1 to 11, as said below
- cutoffs: int32 [4, 128, 4, 6], P(None, 'fsdp'), may hold values from 104 to 254
Outputs:
- new_params: float32 [6144, 16384], P('replica', 'fsdp')
- new_momentum: float32 [6144, 16384], P('replica', 'fsdp')
The draws below stay inside these ranges and needn't reach their ends.
Inputs may be any that keep to these rules, and one draw needn't show every extreme that they name: block_picks[r, o, q, :] holds 1 to 6 different block indices followed by -1 in the remaining slots; in every draw some o and q have 6 indices from every worker r.
All inputs are finite; a program needn't handle non-finite values.
Results may differ from the reference program's by a relative error of at most 0.004.
Values may be sent and summed in bfloat16 or wider, within the bound.
No kernel may reach another device: no remote copies, remote signals or barrier semaphores. Data moves between devices by JAX's collectives and lax.ppermute only.
A program may use at most 64 MiB of HBM per device.

```python
import math
import jax
import jax.numpy as jnp
from jax import lax

BS = 128
D = 6144
FF = 16384
CAP = 6
RPO = 12
CPO = 1
BPO = 12
N_REPLICA = 4
N_FSDP = 128


def draw_pseudo_grads(key, part):
    key_rows, key_cols, key_noise = jax.random.split(key, 3)
    row_pos = jnp.arange(D, dtype=jnp.float32) / max(D - 1, 1)
    col_pos = jnp.arange(FF, dtype=jnp.float32) / max(FF - 1, 1)
    row_spread = 0.3 * jnp.exp(jax.random.uniform(key_rows, (D,), jnp.float32, 0.0, math.log(10.0)))
    col_spread = 0.3 * jnp.exp(jax.random.uniform(key_cols, (FF,), jnp.float32, 0.0, math.log(10.0)))
    base = jax.random.normal(key_noise, (N_REPLICA, D, FF), jnp.float32)
    row_ramp = 1.0 + 0.732 * row_pos
    col_ramp = 1.0 + 2.0 * col_pos
    scale = (row_spread * row_ramp)[:, None] * (col_spread * col_ramp)[None, :] * 0.5
    return (base * scale[None]).astype(jnp.bfloat16)


def shuffled(order_key):
    return jax.random.permutation(order_key, BPO)


def draw_block_picks(key, part):
    key_count, key_owner, key_dest, key_order = jax.random.split(key, 4)
    counts = jax.random.randint(key_count, (N_REPLICA, N_FSDP, N_REPLICA), 1, CAP + 1)
    full_owner = jax.random.randint(key_owner, (), 0, N_FSDP)
    full_dest = jax.random.randint(key_dest, (), 0, N_REPLICA)
    owner_ids = jnp.arange(N_FSDP, dtype=jnp.int32)[None, :, None]
    dest_ids = jnp.arange(N_REPLICA, dtype=jnp.int32)[None, None, :]
    counts = jnp.where((owner_ids == full_owner) & (dest_ids == full_dest), CAP, counts)
    order_keys = jax.random.split(key_order, N_REPLICA * N_FSDP * N_REPLICA)
    orders = jax.vmap(shuffled)(order_keys)[:, :CAP]
    orders = orders.reshape(N_REPLICA, N_FSDP, N_REPLICA, CAP).astype(jnp.int32)
    slots = jnp.arange(CAP, dtype=jnp.int32)
    return jnp.where(slots < counts[..., None], orders, -1).astype(jnp.int32)


def touch_ends(values, own_key, smallest, largest):
    shape = values.shape
    spot = [jax.random.randint(jax.random.fold_in(own_key, axis), (), 0, shape[axis]) for axis in range(len(shape))]
    values = values.at[tuple(spot)].set(smallest)
    longest = shape.index(max(shape))
    spot[longest] = (spot[longest] + 1) % shape[longest]
    return values.at[tuple(spot)].set(largest)


def block_levels(rng, extent, shards, smallest, top_value):
    def one(dim, parts):
        draws = jax.random.uniform(jax.random.fold_in(jax.random.fold_in(rng, 6), dim), (parts,), jnp.float32, smallest / len(shards), top_value / len(shards))
        return jnp.repeat(jnp.exp(draws), extent[dim] // parts).reshape((-1,) + (1,) * (len(extent) - dim - 1))

    gain = one(*shards[0])
    for cut in shards[1:]:
        gain = gain * one(*cut)
    return gain


def scatter_about(own_key, dims, spread, limit, cuts=(), kind=jnp.bfloat16):
    entries = jax.random.normal(own_key, dims, jnp.float32) * spread
    if len(cuts) > 0:
        entries = block_levels(own_key, dims, cuts, -0.22, 0.18) * entries
    return jnp.clip(entries, min=-limit, max=limit).astype(kind)


def setup_inputs(seed: int = 0) -> dict:
    keys = jax.random.split(jax.random.key(seed), 7)
    pseudo_grads = draw_pseudo_grads(jax.random.fold_in(keys[6], 71), 0)
    outer_params = scatter_about(keys[1], (D, FF), 1.0, 6.0, ((0, 4), (1, 128)), jnp.float32)
    momentum = scatter_about(keys[2], (D, FF), 0.1, 0.6, ((0, 4), (1, 128)), jnp.float32)
    clip_level = jnp.clip(jax.random.uniform(keys[3], (1,), jnp.float32, 0.05, 0.2), 0.05, 0.2)
    block_picks = draw_block_picks(jax.random.fold_in(keys[6], 71), 0)
    cutoffs = touch_ends(jax.random.randint(keys[5], (N_REPLICA, N_FSDP, N_REPLICA, CAP), 13 * BS // 16, 2 * BS - 1), jax.random.fold_in(keys[5], 1), 13 * BS // 16, (2 * BS - 1) - 1).astype(jnp.int32)
    return dict(pseudo_grads=pseudo_grads, outer_params=outer_params, momentum=momentum, clip_level=clip_level, block_picks=block_picks, cutoffs=cutoffs)


OUTER_RATE = 0.7
NESTEROV = 0.9
EPSILON = 1e-06
HIGH = lax.Precision.HIGHEST

def cosine_table(length):
    rows_idx = jnp.arange(length, dtype=jnp.float32)[:, None]
    cols_idx = jnp.arange(length, dtype=jnp.float32)[None, :]
    table = jnp.cos(math.pi * (2.0 * cols_idx + 1.0) * rows_idx / (2.0 * length)) * math.sqrt(2.0 / length)
    return jnp.where(rows_idx == 0.0, table * math.sqrt(0.5), table)

def reference(pseudo_grads, outer_params, momentum, clip_level, block_picks, cutoffs):
    table = cosine_table(BS)
    col_width = FF // N_FSDP
    frequency = jnp.arange(BS, dtype=jnp.int32)[:, None] + jnp.arange(BS, dtype=jnp.int32)[None, :]
    block_ids = jnp.arange(BPO, dtype=jnp.int32)

    def owner_sum(owner):
        col_slab = lax.dynamic_slice_in_dim(pseudo_grads, owner * col_width, col_width, 2)
        blocks = col_slab.astype(jnp.float32).reshape(N_REPLICA, N_REPLICA, RPO, BS, CPO, BS)
        blocks = blocks.transpose(0, 1, 2, 4, 3, 5).reshape(N_REPLICA, N_REPLICA, BPO, BS, BS)
        halfway = jnp.einsum('uk,rqbkl->rqbul', table, blocks, precision=HIGH)
        coefficients = jnp.einsum('rqbul,vl->rqbuv', halfway, table, precision=HIGH)
        own_picks = lax.dynamic_index_in_dim(block_picks, owner, 1, keepdims=False)
        own_cuts = lax.dynamic_index_in_dim(cutoffs, owner, 1, keepdims=False)
        pick_hit = own_picks[..., None] == block_ids
        block_cut = lax.optimization_barrier(jnp.max(jnp.where(pick_hit, own_cuts[..., None], -1), axis=2))
        keep_mask = frequency <= block_cut[..., None, None]
        return lax.optimization_barrier(jnp.sum(jnp.where(keep_mask, coefficients, jnp.float32(0.0)), axis=0))
    summed = lax.map(owner_sum, jnp.arange(N_FSDP, dtype=jnp.int32))
    square_total = jnp.sum(summed * summed)
    factor = jnp.minimum(jnp.float32(1.0), clip_level[0] * math.sqrt(D * FF) / (jnp.sqrt(square_total) + EPSILON))

    def owner_back(scaled):
        halfway = jnp.einsum('uk,qbuv->qbkv', table, scaled, precision=HIGH)
        return jnp.einsum('qbkv,vl->qbkl', halfway, table, precision=HIGH)
    spatial = lax.map(owner_back, summed * factor)
    spatial = spatial.reshape(N_FSDP, N_REPLICA, RPO, CPO, BS, BS)
    update = spatial.transpose(1, 2, 4, 0, 3, 5).reshape(D, FF)
    new_momentum = NESTEROV * momentum + update
    new_params = outer_params - OUTER_RATE * (update + NESTEROV * new_momentum)
    return (new_params, new_momentum)
```

```python
import math

import jax
import jax.numpy as jnp
import ml_dtypes
import numpy as np
from jax import lax
from jax.experimental import pallas as pl
from jax.experimental.pallas import tpu as pltpu
from jax.sharding import Mesh, PartitionSpec as P

BS = 128
D = 6144
FF = 16384
OUTER_RATE = 0.7
NESTEROV = 0.9
EPSILON = 1e-06
NX, NY, NZ, NC = 4, 4, 16, 2
BPO = 12
TAIL = 16
F32 = jnp.float32
BF16 = jnp.bfloat16


def table_parts():
    u = np.arange(BS, dtype=np.float64)[:, None]
    k = np.arange(BS, dtype=np.float64)[None, :]
    c = np.cos(math.pi * (2.0 * k + 1.0) * u / (2.0 * BS)) * math.sqrt(2.0 / BS)
    c[0] *= math.sqrt(0.5)
    hi = c.astype(ml_dtypes.bfloat16)
    lo = (c - hi.astype(np.float64)).astype(ml_dtypes.bfloat16)
    return hi, lo


def dot(a, b):
    return lax.dot_general(a, b, (((1,), (0,)), ((), ())), preferred_element_type=F32)


def split(v):
    hi = v.astype(BF16)
    return hi, (v - hi.astype(F32)).astype(BF16)


def times_wide(v, wide):
    hi, lo = split(v)
    both = dot(hi, wide)
    return both[:, :BS] + both[:, BS:] + dot(lo, wide[:, :BS])


def tall_times(tall, v):
    hi, lo = split(v)
    both = dot(tall, hi)
    return both[:BS] + both[BS:] + dot(tall[:BS], lo)


def pack_kernel(pos, g, out):
    c = pos[1]
    for cc in range(2):
        core = c if cc == 0 else 1 - c
        for m in range(4):
            for w in range(4):
                start = pl.multiple_of((2 * (4 * w + m) + core) * BS, BS)
                out[0, cc, 4 * m + w] = g[:, pl.ds(start, BS)]


def by_place(pos, mine, other, body):
    for p in range(4):
        for c in range(2):

            @pl.when((pos[0] == p) & (pos[1] == c))
            def _(p=p, c=c):
                if c == 0:
                    body(p, mine, other)
                else:
                    body(p, other, mine)


def exchange_kernel(pos, mine, other, a, b):
    def body(p, lo, hi):
        if p in (0, 3):
            s = slice(0, 4) if p == 0 else slice(12, 16)
            a[:, :, 0:48] = lo[:, s]
            a[:, :, 48:96] = hi[:, s]
            return
        for k in range(3):
            if p == 1:
                a[:, :, 32 * k : 32 * k + 32] = lo[:, 4 * k + 4 : 4 * k + 8, 0:32]
            else:
                a[:, :, 32 * k : 32 * k + 32] = hi[:, 4 * k : 4 * k + 4, 16:48]
        if p == 1:
            b[:, :, 0:16] = lo[:, 0:8, 32:48]
            b[:, :, 16:64] = hi[:, 0:8]
        else:
            b[:, :, 0:48] = lo[:, 8:16]
            b[:, :, 48:64] = hi[:, 8:16, 0:16]

    by_place(pos, mine, other, body)


def assemble(pos, mine, other, a, b, x):
    def body(p, lo, hi):
        for k in range(3):
            m = k + (k >= p)
            d = slice(4 * k, 4 * k + 4)
            s = slice(4 * m, 4 * m + 4)
            third = slice(32 * k, 32 * k + 32)
            if p == 0:
                x[:, d, 0:48] = lo[:, s]
                x[:, d, 48:96] = hi[:, s]
                x[:, d, 96:128] = a[:, :, third]
            elif p == 3:
                x[:, d, 0:32] = a[:, :, third]
                x[:, d, 32:80] = lo[:, s]
                x[:, d, 80:128] = hi[:, s]
            elif p == 1 and m == 0:
                x[:, d, 0:96] = a[:, :, :]
                x[:, d, 96:128] = lo[:, s, 0:32]
            elif p == 1:
                x[:, d, 0:16] = lo[:, s, 32:48]
                x[:, d, 16:64] = hi[:, s]
                x[:, d, 64:128] = b[:, 4 * (m - 2) : 4 * (m - 2) + 4]
            elif m == 3:
                x[:, d, 0:32] = hi[:, s, 16:48]
                x[:, d, 32:128] = a[:, :, :]
            else:
                x[:, d, 0:64] = b[:, s]
                x[:, d, 64:112] = lo[:, s]
                x[:, d, 112:128] = hi[:, s, 0:16]

    by_place(pos, mine, other, body)


def exponent(size):
    return jnp.clip(jnp.floor(jnp.log2(jnp.maximum(size, F32(1e-30)))) + 1.0, -100.0, 200.0)


def forward_kernel(pos, cut, mine, other, a, b, tall, wide, out, x, exps):
    assemble(pos, mine, other, a, b, x)
    p = pos[0]
    freq = lax.broadcasted_iota(jnp.int32, (BS, BS), 0) + lax.broadcasted_iota(jnp.int32, (BS, BS), 1)
    exps[...] = jnp.zeros_like(exps)
    for w in range(4):
        out[4 * w + p, 0:BS] = jnp.zeros((BS, BS), jnp.int16)

    def step(i, square):
        k = i // 4
        m = k + (k >= p).astype(jnp.int32)
        blk = p - (p > m).astype(jnp.int32)
        zq = 4 * (i % 4) + m
        total = jnp.zeros((BS, BS), F32)
        for r in range(NX):
            both = dot(x[r, i], wide[...])
            coef = tall_times(tall[...], both[:, :BS] + both[:, BS:])
            total += jnp.where(freq <= cut[zq, 4 * blk + r], coef, 0.0)
        e = exponent(jnp.max(jnp.abs(total), axis=0, keepdims=True))
        code = jnp.clip(jnp.floor(total * jnp.exp2(15.0 - e) + 0.5), -32767.0, 32767.0)
        out[zq, 0:BS] = code.astype(jnp.int32).astype(jnp.int16)
        exps[pl.ds(zq, 1), :] = e
        return square + jnp.sum(total * total, axis=0, keepdims=True)

    square = lax.fori_loop(0, BPO, step, jnp.zeros((1, BS), F32))
    e = exponent(square)
    scaled = jnp.minimum(square, F32(3e38)) * jnp.exp2(-0.5 * e) * jnp.exp2(-0.5 * e) * 16384.0
    d1 = jnp.floor(scaled)
    d2 = jnp.floor((scaled - d1) * 16384.0)
    e = jnp.where(square > F32(3e38), 200.0, e)
    row = lax.broadcasted_iota(jnp.int32, (TAIL, BS), 0)
    tail = jnp.where(row == 1, e, jnp.where(row == 2, d1, jnp.where(row == 3, d2, 0.0)))
    for s in range(NZ):
        mix = jnp.where(row == 0, exps[s : s + 1, :], tail)
        out[s, BS : BS + TAIL] = mix.astype(jnp.int32).astype(jnp.int16)


def compact_kernel(pos, z, out, norm):
    p = pos[0]
    row = lax.broadcasted_iota(jnp.int32, (TAIL, BS), 0)
    tail = jnp.zeros((TAIL, BS), F32)
    for g in range(4):
        for blk in range(3):
            src = 4 * g + blk + (p <= blk).astype(jnp.int32)
            n = 3 * g + blk
            out[BS * n : BS * n + BS] = z[src, 0:BS]
            e = z[src, BS : BS + TAIL].astype(jnp.int32).astype(F32)[0:1]
            tail = jnp.where(row == n, e, tail)
    out[BS * BPO : BS * BPO + TAIL] = tail.astype(jnp.int32).astype(jnp.int16)
    total = jnp.zeros((1, BS), F32)
    for s in range(NZ):
        t = z[s, BS : BS + TAIL].astype(jnp.int32).astype(F32)
        part = t[2:3] * F32(1.0 / 16384.0) + t[3:4] * F32(1.0 / 16384.0**2)
        total += part * jnp.exp2(0.5 * t[1:2]) * jnp.exp2(0.5 * t[1:2])
    norm[...] = jnp.broadcast_to(total[None], norm.shape)


def update_kernel(code, tail, norm, clip, params, mom, tall, wide, new_p, new_m):
    i = pl.program_id(0)
    total = jnp.sum(jnp.sum(norm[...], axis=0), axis=1, keepdims=True)
    factor = jnp.minimum(F32(1.0), clip[0] * F32(math.sqrt(D * FF)) / (jnp.sqrt(total) + F32(EPSILON)))
    row = lax.broadcasted_iota(jnp.int32, (TAIL, BS), 0)
    exps = tail[...].astype(jnp.int32).astype(F32)
    per = code.shape[0] // BS
    for n in range(per):
        e = jnp.sum(jnp.where(row == per * i + n, exps, 0.0), axis=0, keepdims=True)
        d = slice(BS * n, BS * n + BS)
        coef = code[d].astype(jnp.int32).astype(F32) * (jnp.exp2(e - 15.0) * factor)
        upd = tall_times(tall[...], times_wide(coef, wide[...]))
        nm = NESTEROV * mom[d] + upd
        new_m[d] = nm
        new_p[d] = params[d] - OUTER_RATE * (upd + NESTEROV * nm)


SMEM = pl.BlockSpec(memory_space=pltpu.SMEM)
VMEM = pl.BlockSpec(memory_space=pltpu.VMEM)
BIG = pltpu.CompilerParams(vmem_limit_bytes=40 * 1024 * 1024)


def per_device(pseudo_grads, outer_params, momentum, clip_level, block_picks, cutoffs):
    z = lax.axis_index("z")
    pos = jnp.stack([z % 4, lax.axis_index("c")]).astype(jnp.int32)
    hi, lo = table_parts()
    fwd_wide = jnp.asarray(np.concatenate([hi.T, lo.T], axis=1))
    fwd_tall = jnp.asarray(np.concatenate([hi, lo], axis=0))
    inv_wide = jnp.asarray(np.concatenate([hi, lo], axis=1))
    inv_tall = jnp.asarray(np.concatenate([hi.T, lo.T], axis=0))
    rows = pseudo_grads.shape[1]

    packed = pl.pallas_call(
        pack_kernel,
        out_shape=jax.ShapeDtypeStruct((NY, NC, NZ, rows, BS), BF16),
        grid=(NY,),
        in_specs=[SMEM, pl.BlockSpec((None, rows, FF // NY), lambda j: (0, 0, j))],
        out_specs=pl.BlockSpec((1, NC, NZ, rows, BS), lambda j: (j, 0, 0, 0, 0)),
        compiler_params=BIG,
        name="pack",
    )(pos, pseudo_grads)
    spread = lax.all_to_all(packed, "x", 0, 0, tiled=True)
    other = lax.ppermute(spread[:, 1], "c", [(0, 1), (1, 0)])

    half = pl.BlockSpec((NX, None, NZ, rows, BS), lambda i: (0, 0, 0, 0, 0))
    a, b = pl.pallas_call(
        exchange_kernel,
        out_shape=(
            jax.ShapeDtypeStruct((NX, 4, 96, BS), BF16),
            jax.ShapeDtypeStruct((NX, 8, 64, BS), BF16),
        ),
        grid=(1,),
        in_specs=[SMEM, half, VMEM],
        out_specs=(VMEM, VMEM),
        compiler_params=BIG,
        name="exchange",
    )(pos, spread, other)

    hit = block_picks[:, 0, :, :, None] == jnp.arange(BPO, dtype=jnp.int32)
    cut = jnp.max(jnp.where(hit, cutoffs[:, 0, :, :, None], -1), axis=2)
    cut = cut.transpose(1, 2, 0).reshape(NY, 4, 1, 12)
    cut = jnp.broadcast_to(cut, (NY, 4, 4, 12)).reshape(NY * NZ, 1, 12)
    cut = jnp.pad(cut, ((0, 0), (0, 0), (0, BS - 12)))
    cut, a, b = lax.optimization_barrier((cut, a, b))

    pair_a, pair_b = [], []
    for g in range(0, NZ, 4):
        pair_a += [(g, g + 1), (g + 1, g), (g + 2, g + 3), (g + 3, g + 2)]
        pair_b += [(g + 1, g + 2), (g + 2, g + 1)]
    a = lax.ppermute(a, "z", pair_a)
    b = lax.ppermute(b, "z", pair_b)
    cut = lax.all_to_all(cut, ("y", "z"), 0, 0, tiled=True)
    cut = lax.dynamic_slice_in_dim(cut[:, 0], lax.axis_index("x") * NZ, NZ, 0)

    coded = pl.pallas_call(
        forward_kernel,
        out_shape=jax.ShapeDtypeStruct((NZ, BS + TAIL, BS), jnp.int16),
        grid=(1,),
        in_specs=[SMEM, SMEM, half, VMEM, VMEM, VMEM, VMEM, VMEM],
        out_specs=VMEM,
        scratch_shapes=[
            pltpu.VMEM((NX, BPO, BS, BS), BF16),
            pltpu.VMEM((NZ, BS), F32),
        ],
        compiler_params=BIG,
        name="forward",
    )(pos, cut, spread, other, a, b, fwd_tall, fwd_wide)
    coded = lax.all_to_all(coded, "z", 0, 0, tiled=True)

    coded, norm = pl.pallas_call(
        compact_kernel,
        out_shape=(
            jax.ShapeDtypeStruct((BPO * BS + TAIL, BS), jnp.int16),
            jax.ShapeDtypeStruct((NX * NY * NC, 1, BS), F32),
        ),
        in_specs=[SMEM, VMEM],
        out_specs=(VMEM, VMEM),
        compiler_params=BIG,
        name="compact",
    )(pos, coded)
    swap = [(NY * i + j, NX * j + i) for i in range(NX) for j in range(NY)]
    coded = lax.ppermute(coded, ("x", "y"), swap)
    norm = lax.all_to_all(norm, ("x", "y", "c"), 0, 0, tiled=True)

    per = 3
    steps = BPO // per
    tile = pl.BlockSpec((per * BS, BS), lambda i: (i, 0))

    def whole(*shape):
        return pl.BlockSpec(shape, lambda i: (0,) * len(shape))

    return pl.pallas_call(
        update_kernel,
        out_shape=(
            jax.ShapeDtypeStruct(outer_params.shape, F32),
            jax.ShapeDtypeStruct(outer_params.shape, F32),
        ),
        grid=(steps,),
        in_specs=[
            tile,
            pl.BlockSpec((TAIL, BS), lambda i: (BPO * BS // TAIL, 0)),
            whole(NX * NY * NC, 1, BS),
            SMEM,
            tile,
            tile,
            whole(2 * BS, BS),
            whole(BS, 2 * BS),
        ],
        out_specs=(tile, tile),
        compiler_params=BIG,
        name="update",
    )(coded, coded, norm, clip_level, outer_params, momentum, inv_tall, inv_wide)


def solution(mesh):
    grid = Mesh(mesh.devices.reshape(NX, NY, NZ, NC), ("x", "y", "z", "c"))
    yzc = ("y", "z", "c")
    in_specs = (P("x", yzc, None), P("x", yzc), P("x", yzc), P(), P(None, yzc, None, None), P(None, yzc, None, None))
    out_specs = (P("x", yzc), P("x", yzc))
    return jax.shard_map(per_device, mesh=grid, in_specs=in_specs, out_specs=out_specs, check_vma=False)
```

```python
import functools
import math

import jax
import jax.numpy as jnp
import ml_dtypes
import numpy as np
from jax import lax
from jax.experimental import pallas as pl
from jax.experimental.pallas import tpu as pltpu
from jax.sharding import Mesh, PartitionSpec as P

BS = 128
D = 6144
FF = 16384
OUTER_RATE = 0.7
NESTEROV = 0.9
EPSILON = 1e-06
NX, NY, NZ, NC = 4, 4, 16, 2
BPO = 12
TAIL = 16
F32 = jnp.float32
BF16 = jnp.bfloat16


def table_parts():
    u = np.arange(BS, dtype=np.float64)[:, None]
    k = np.arange(BS, dtype=np.float64)[None, :]
    c = np.cos(math.pi * (2.0 * k + 1.0) * u / (2.0 * BS)) * math.sqrt(2.0 / BS)
    c[0] *= math.sqrt(0.5)
    hi = c.astype(ml_dtypes.bfloat16)
    lo = (c - hi.astype(np.float64)).astype(ml_dtypes.bfloat16)
    return hi, lo


def dot(a, b):
    return lax.dot_general(a, b, (((1,), (0,)), ((), ())), preferred_element_type=F32)


def split(v):
    hi = v.astype(BF16)
    return hi, (v - hi.astype(F32)).astype(BF16)


def times_wide(v, wide):
    hi, lo = split(v)
    both = dot(hi, wide)
    return both[:, :BS] + both[:, BS:] + dot(lo, wide[:, :BS])


def tall_times(tall, v):
    hi, lo = split(v)
    both = dot(tall, hi)
    return both[:BS] + both[BS:] + dot(tall[:BS], lo)


def pack_kernel(pos, g, out):
    c = pos[1]
    for cc in range(2):
        core = c if cc == 0 else 1 - c
        for m in range(4):
            for w in range(4):
                start = pl.multiple_of((2 * (4 * w + m) + core) * BS, BS)
                out[0, cc, 4 * m + w] = g[:, pl.ds(start, BS)]


def by_place(pos, mine, other, body):
    mine = mine.at[:, 0]
    for p in range(4):
        for c in range(2):

            @pl.when((pos[0] == p) & (pos[1] == c))
            def _(p=p, c=c):
                if c == 0:
                    body(p, mine, other)
                else:
                    body(p, other, mine)


def exchange_kernel(pos, mine, other, a, b):
    def body(p, lo, hi):
        if p in (0, 3):
            s = slice(0, 4) if p == 0 else slice(12, 16)
            a[:, :, 0:48] = lo[:, s]
            a[:, :, 48:96] = hi[:, s]
            return
        for k in range(3):
            if p == 1:
                a[:, :, 32 * k : 32 * k + 32] = lo[:, 4 * k + 4 : 4 * k + 8, 0:32]
            else:
                a[:, :, 32 * k : 32 * k + 32] = hi[:, 4 * k : 4 * k + 4, 16:48]
        if p == 1:
            b[:, :, 0:16] = lo[:, 0:8, 32:48]
            b[:, :, 16:64] = hi[:, 0:8]
        else:
            b[:, :, 0:48] = lo[:, 8:16]
            b[:, :, 48:64] = hi[:, 8:16, 0:16]

    by_place(pos, mine, other, body)


def assemble(k, pos, mine, other, a, b, x):
    def body(p, lo, hi):
        m = k + (k >= p)
        s = slice(4 * m, 4 * m + 4)
        third = slice(32 * k, 32 * k + 32)
        if p == 0:
            x[:, :, 0:48] = lo[:, s]
            x[:, :, 48:96] = hi[:, s]
            x[:, :, 96:128] = a[:, :, third]
        elif p == 3:
            x[:, :, 0:32] = a[:, :, third]
            x[:, :, 32:80] = lo[:, s]
            x[:, :, 80:128] = hi[:, s]
        elif p == 1 and m == 0:
            x[:, :, 0:96] = a[:, :, :]
            x[:, :, 96:128] = lo[:, s, 0:32]
        elif p == 1:
            x[:, :, 0:16] = lo[:, s, 32:48]
            x[:, :, 16:64] = hi[:, s]
            x[:, :, 64:128] = b[:, 4 * (m - 2) : 4 * (m - 2) + 4]
        elif m == 3:
            x[:, :, 0:32] = hi[:, s, 16:48]
            x[:, :, 32:128] = a[:, :, :]
        else:
            x[:, :, 0:64] = b[:, s]
            x[:, :, 64:112] = lo[:, s]
            x[:, :, 112:128] = hi[:, s, 0:16]

    by_place(pos, mine, other, body)


def exponent(size):
    return jnp.clip(jnp.floor(jnp.log2(jnp.maximum(size, F32(1e-30)))) + 1.0, -100.0, 200.0)


def forward_kernel(k, pos, cut, mine, other, a, b, tall, wide, out, square, x):
    assemble(k, pos, mine, other, a, b, x)
    p = pos[0]
    m = k + (k >= p).astype(jnp.int32)
    blk = p - (p > m).astype(jnp.int32)
    freq = lax.broadcasted_iota(jnp.int32, (BS, BS), 0) + lax.broadcasted_iota(jnp.int32, (BS, BS), 1)
    row = lax.broadcasted_iota(jnp.int32, (TAIL, BS), 0)
    tail = jnp.zeros((TAIL, BS), F32)
    squares = jnp.zeros((1, BS), F32)
    for w in range(4):
        total = jnp.zeros((BS, BS), F32)
        for r in range(NX):
            both = dot(x[r, w], wide[...])
            hi, lo = split(both[:, :BS] + both[:, BS:])
            four = dot(tall[...], jnp.concatenate([hi, lo], axis=1))
            coef = four[:BS, :BS] + (four[BS:, :BS] + four[:BS, BS:])
            total += jnp.where(freq <= cut[4 * w + m, 4 * blk + r], coef, 0.0)
        e = exponent(jnp.max(jnp.abs(total), axis=0, keepdims=True))
        code = jnp.clip(jnp.floor(total * jnp.exp2(15.0 - e) + 0.5), -32767.0, 32767.0)
        out[BS * w : BS * w + BS] = code.astype(jnp.int32).astype(jnp.int16)
        tail = jnp.where(row == w, e, tail)
        squares += jnp.sum(total * total, axis=0, keepdims=True)
    out[4 * BS : 4 * BS + TAIL] = tail.astype(jnp.int32).astype(jnp.int16)
    square[...] = squares


def slots_kernel(pos, c0, c1, c2, norm, out):
    p = pos[0]
    square = jnp.sum(norm[...], axis=0)
    e = exponent(square)
    scaled = jnp.minimum(square, F32(3e38)) * jnp.exp2(-0.5 * e) * jnp.exp2(-0.5 * e) * 16384.0
    d1 = jnp.floor(scaled)
    d2 = jnp.floor((scaled - d1) * 16384.0)
    e = jnp.where(square > F32(3e38), 200.0, e)
    row = lax.broadcasted_iota(jnp.int32, (TAIL, BS), 0)
    tail = jnp.where(row == 1, e, jnp.where(row == 2, d1, jnp.where(row == 3, d2, 0.0)))
    for k in range(3):
        code = (c0, c1, c2)[k]
        m = k + (k >= p).astype(jnp.int32)
        exps = code[4 * BS : 4 * BS + TAIL].astype(jnp.int32).astype(F32)
        for w in range(4):
            out[4 * w + m, 0:BS] = code[BS * w : BS * w + BS]
            mix = jnp.where(row == 0, exps[w : w + 1], tail)
            out[4 * w + m, BS : BS + TAIL] = mix.astype(jnp.int32).astype(jnp.int16)
    tail = tail.astype(jnp.int32).astype(jnp.int16)
    for w in range(4):
        out[4 * w + p, 0:BS] = jnp.zeros((BS, BS), jnp.int16)
        out[4 * w + p, BS : BS + TAIL] = tail


def update_kernel(pos, z, clip, params, mom, tall, wide, new_p, new_m):
    g = pl.program_id(0)
    p = pos[0]
    total = jnp.zeros((1, BS), F32)
    for s in range(NZ):
        t = z[s, BS : BS + TAIL].astype(jnp.int32).astype(F32)
        part = t[2:3] * F32(1.0 / 16384.0) + t[3:4] * F32(1.0 / 16384.0**2)
        total += part * jnp.exp2(0.5 * t[1:2]) * jnp.exp2(0.5 * t[1:2])
    total = jnp.sum(total, axis=1, keepdims=True)
    factor = jnp.minimum(F32(1.0), clip[0] * F32(math.sqrt(D * FF)) / (jnp.sqrt(total) + F32(EPSILON)))
    for n in range(3):
        src = 4 * g + n + (p <= n).astype(jnp.int32)
        e = z[src, BS : BS + TAIL].astype(jnp.int32).astype(F32)[0:1]
        d = slice(BS * n, BS * n + BS)
        coef = z[src, 0:BS].astype(jnp.int32).astype(F32) * (jnp.exp2(e - 15.0) * factor)
        upd = tall_times(tall[...], times_wide(coef, wide[...]))
        nm = NESTEROV * mom[d] + upd
        new_m[d] = nm
        new_p[d] = params[d] - OUTER_RATE * (upd + NESTEROV * nm)


SMEM = pl.BlockSpec(memory_space=pltpu.SMEM)
VMEM = pl.BlockSpec(memory_space=pltpu.VMEM)
BIG = pltpu.CompilerParams(vmem_limit_bytes=40 * 1024 * 1024)


def call(kernel, out_shape, inputs, name, scratch=()):
    return pl.pallas_call(
        kernel,
        out_shape=out_shape,
        in_specs=[SMEM if i.dtype == jnp.int32 else VMEM for i in inputs],
        out_specs=jax.tree.map(lambda _: VMEM, out_shape),
        scratch_shapes=scratch,
        compiler_params=BIG,
        name=name,
    )(*inputs)


def per_device(pseudo_grads, outer_params, momentum, clip_level, block_picks, cutoffs):
    z = lax.axis_index("z")
    pos = jnp.stack([z % 4, lax.axis_index("c")]).astype(jnp.int32)
    hi, lo = table_parts()
    fwd_wide = jnp.asarray(np.concatenate([hi.T, lo.T], axis=1))
    fwd_tall = jnp.asarray(np.concatenate([hi, lo], axis=0))
    inv_wide = jnp.asarray(np.concatenate([hi, lo], axis=1))
    inv_tall = jnp.asarray(np.concatenate([hi.T, lo.T], axis=0))
    rows = pseudo_grads.shape[1]
    swap = [(NY * i + j, NX * j + i) for i in range(NX) for j in range(NY)]
    shape = jax.ShapeDtypeStruct

    picks, cuts = (
        lax.dynamic_index_in_dim(v[:, 0], lax.axis_index("x"), 1, keepdims=False) for v in (block_picks, cutoffs)
    )
    hit = picks[:, :, None] == jnp.arange(BPO, dtype=jnp.int32)
    cut = jnp.max(jnp.where(hit, cuts[:, :, None], -1), axis=1)
    cut = jnp.pad(cut.T.reshape(4, BPO), ((0, 4), (0, BS - BPO)))
    cut = lax.ppermute(cut, ("x", "y"), swap)

    packed = pl.pallas_call(
        pack_kernel,
        out_shape=shape((NY, NC, NZ, rows, BS), BF16),
        grid=(NY,),
        in_specs=[SMEM, pl.BlockSpec((None, rows, FF // NY), lambda j: (0, 0, j))],
        out_specs=pl.BlockSpec((1, NC, NZ, rows, BS), lambda j: (j, 0, 0, 0, 0)),
        compiler_params=BIG,
        name="pack",
    )(pos, pseudo_grads)
    spread = lax.all_to_all(packed, "x", 0, 0, tiled=True)
    other = lax.ppermute(spread[:, 1], "c", [(0, 1), (1, 0)])

    a, b = call(
        exchange_kernel,
        (shape((NX, 4, 96, BS), BF16), shape((NX, 8, 64, BS), BF16)),
        (pos, spread, other),
        "exchange",
    )
    cut = jnp.broadcast_to(cut[:4, None], (4, 4, BS)).reshape(NZ, 1, BS)
    cut, a, b = lax.optimization_barrier((cut, a, b))
    pair_a, pair_b = [], []
    for g in range(0, NZ, 4):
        pair_a += [(g, g + 1), (g + 1, g), (g + 2, g + 3), (g + 3, g + 2)]
        pair_b += [(g + 1, g + 2), (g + 2, g + 1)]
    a = lax.ppermute(a, "z", pair_a)
    b = lax.ppermute(b, "z", pair_b)
    cut = lax.all_to_all(cut, "z", 0, 0, tiled=True)[:, 0]

    parts, squares = [], []
    for k in range(3):
        code, square = call(
            functools.partial(forward_kernel, k),
            (shape((4 * BS + TAIL, BS), jnp.int16), shape((1, BS), F32)),
            (pos, cut, spread, other, a, b, fwd_tall, fwd_wide),
            "forward",
            [pltpu.VMEM((NX, 4, BS, BS), BF16)],
        )
        parts.append(lax.ppermute(code, ("x", "y"), swap))
        squares.append(square)
    norm = jnp.broadcast_to(sum(squares)[None], (NX * NY * NC, 1, BS))
    norm = lax.all_to_all(norm, ("x", "y", "c"), 0, 0, tiled=True)
    coded = call(slots_kernel, shape((NZ, BS + TAIL, BS), jnp.int16), (pos, *parts, norm), "slots")
    coded = lax.all_to_all(coded, "z", 0, 0, tiled=True)

    tile = pl.BlockSpec((3 * BS, BS), lambda i: (i, 0))
    return pl.pallas_call(
        update_kernel,
        out_shape=(shape(outer_params.shape, F32), shape(outer_params.shape, F32)),
        grid=(4,),
        in_specs=[SMEM, VMEM, SMEM, tile, tile, VMEM, VMEM],
        out_specs=(tile, tile),
        compiler_params=BIG,
        name="update",
    )(pos, coded, clip_level, outer_params, momentum, inv_tall, inv_wide)


def solution(mesh):
    grid = Mesh(mesh.devices.reshape(NX, NY, NZ, NC), ("x", "y", "z", "c"))
    yzc = ("y", "z", "c")
    in_specs = (P("x", yzc, None), P("x", yzc), P("x", yzc), P(), P(None, yzc, None, None), P(None, yzc, None, None))
    out_specs = (P("x", yzc), P("x", yzc))
    return jax.shard_map(per_device, mesh=grid, in_specs=in_specs, out_specs=out_specs, check_vma=False)
```

```python
import functools
import math

import jax
import jax.numpy as jnp
import ml_dtypes
import numpy as np
from jax import lax
from jax.experimental import pallas as pl
from jax.experimental.pallas import tpu as pltpu
from jax.sharding import Mesh, PartitionSpec as P

BS = 128
D = 6144
FF = 16384
OUTER_RATE = 0.7
NESTEROV = 0.9
EPSILON = 1e-06
NX, NY, NZ, NC = 4, 4, 16, 2
BPO = 12
TAIL = 16
F32 = jnp.float32
BF16 = jnp.bfloat16


def table_parts():
    u = np.arange(BS, dtype=np.float64)[:, None]
    k = np.arange(BS, dtype=np.float64)[None, :]
    c = np.cos(math.pi * (2.0 * k + 1.0) * u / (2.0 * BS)) * math.sqrt(2.0 / BS)
    c[0] *= math.sqrt(0.5)
    hi = c.astype(ml_dtypes.bfloat16)
    lo = (c - hi.astype(np.float64)).astype(ml_dtypes.bfloat16)
    return hi, lo


def dot(a, b):
    return lax.dot_general(a, b, (((1,), (0,)), ((), ())), preferred_element_type=F32)


def split(v):
    hi = v.astype(BF16)
    return hi, (v - hi.astype(F32)).astype(BF16)


def times_wide(v, wide):
    hi, lo = split(v)
    both = dot(hi, wide)
    return both[:, :BS] + both[:, BS:] + dot(lo, wide[:, :BS])


def tall_times(tall, v):
    hi, lo = split(v)
    both = dot(tall, hi)
    return both[:BS] + both[BS:] + dot(tall[:BS], lo)


def pack_kernel(pos, g, out):
    c = pos[1]
    for cc in range(2):
        core = c if cc == 0 else 1 - c
        for m in range(4):
            for w in range(4):
                start = pl.multiple_of((2 * (4 * w + m) + core) * BS, BS)
                out[0, cc, 4 * m + w] = g[:, pl.ds(start, BS)]


def by_place(pos, mine, other, body):
    mine = mine.at[:, 0]
    for p in range(4):
        for c in range(2):

            @pl.when((pos[0] == p) & (pos[1] == c))
            def _(p=p, c=c):
                if c == 0:
                    body(p, mine, other)
                else:
                    body(p, other, mine)


def exchange_kernel(pos, mine, other, a, b):
    def body(p, lo, hi):
        if p in (0, 3):
            s = slice(0, 4) if p == 0 else slice(12, 16)
            a[:, :, 0:48] = lo[:, s]
            a[:, :, 48:96] = hi[:, s]
            return
        for k in range(3):
            if p == 1:
                a[:, :, 32 * k : 32 * k + 32] = lo[:, 4 * k + 4 : 4 * k + 8, 0:32]
            else:
                a[:, :, 32 * k : 32 * k + 32] = hi[:, 4 * k : 4 * k + 4, 16:48]
        if p == 1:
            b[:, :, 0:16] = lo[:, 0:8, 32:48]
            b[:, :, 16:64] = hi[:, 0:8]
        else:
            b[:, :, 0:48] = lo[:, 8:16]
            b[:, :, 48:64] = hi[:, 8:16, 0:16]

    by_place(pos, mine, other, body)


def assemble(pos, mine, other, a, b, whole):
    def place(p, k, lo, hi, x):
        m = k + (k >= p)
        s = slice(4 * m, 4 * m + 4)
        third = slice(32 * k, 32 * k + 32)
        if p == 0:
            x[:, :, 0:48] = lo[:, s]
            x[:, :, 48:96] = hi[:, s]
            x[:, :, 96:128] = a[:, :, third]
        elif p == 3:
            x[:, :, 0:32] = a[:, :, third]
            x[:, :, 32:80] = lo[:, s]
            x[:, :, 80:128] = hi[:, s]
        elif p == 1 and m == 0:
            x[:, :, 0:96] = a[:, :, :]
            x[:, :, 96:128] = lo[:, s, 0:32]
        elif p == 1:
            x[:, :, 0:16] = lo[:, s, 32:48]
            x[:, :, 16:64] = hi[:, s]
            x[:, :, 64:128] = b[:, 4 * (m - 2) : 4 * (m - 2) + 4]
        elif m == 3:
            x[:, :, 0:32] = hi[:, s, 16:48]
            x[:, :, 32:128] = a[:, :, :]
        else:
            x[:, :, 0:64] = b[:, s]
            x[:, :, 64:112] = lo[:, s]
            x[:, :, 112:128] = hi[:, s, 0:16]

    def body(p, lo, hi):
        for k in range(3):
            place(p, k, lo, hi, whole.at[:, 4 * k : 4 * k + 4])

    by_place(pos, mine, other, body)


def exponent(size):
    return jnp.clip(jnp.floor(jnp.log2(jnp.maximum(size, F32(1e-30)))) + 1.0, -100.0, 200.0)


def forward_kernel(pos, cut, mine, other, a, b, tall, wide, out, x, exps):
    assemble(pos, mine, other, a, b, x)
    p, grp = pos[0], pos[2]
    freq = lax.broadcasted_iota(jnp.int32, (BS, BS), 0) + lax.broadcasted_iota(jnp.int32, (BS, BS), 1)
    row = lax.broadcasted_iota(jnp.int32, (TAIL, BS), 0)
    exps[...] = jnp.zeros_like(exps)
    for w in range(4):
        out[4 * w + p, 0:BS] = jnp.zeros((BS, BS), jnp.int16)

    def step(w, square):
        for k in range(3):
            m = k + (k >= p).astype(jnp.int32)
            blk = p - (p > m).astype(jnp.int32)
            src = 4 * ((grp + 4 - w) % 4) + (p + 4 - m) % 4
            total = jnp.zeros((BS, BS), F32)
            for r in range(NX):
                both = dot(x[r, 4 * k + w], wide[...])
                hi, lo = split(both[:, :BS] + both[:, BS:])
                four = dot(tall[...], jnp.concatenate([hi, lo], axis=1))
                coef = four[:BS, :BS] + (four[BS:, :BS] + four[:BS, BS:])
                total += jnp.where(freq <= cut[src, 4 * blk + r], coef, 0.0)
            e = exponent(jnp.max(jnp.abs(total), axis=0, keepdims=True))
            code = jnp.clip(jnp.floor(total * jnp.exp2(15.0 - e) + 0.5), -32767.0, 32767.0)
            out[4 * w + m, 0:BS] = code.astype(jnp.int32).astype(jnp.int16)
            exps[pl.ds(4 * w + m, 1), :] = e
            square += jnp.sum(total * total, axis=0, keepdims=True)
        return square

    square = lax.fori_loop(0, 4, step, jnp.zeros((1, BS), F32))
    e = exponent(square)
    scaled = jnp.minimum(square, F32(3e38)) * jnp.exp2(-0.5 * e) * jnp.exp2(-0.5 * e) * 16384.0
    d1 = jnp.floor(scaled)
    d2 = jnp.floor((scaled - d1) * 16384.0)
    e = jnp.where(square > F32(3e38), 200.0, e)
    tail = jnp.where(row == 1, e, jnp.where(row == 2, d1, jnp.where(row == 3, d2, 0.0)))
    for s in range(NZ):
        mix = jnp.where(row == 0, exps[s : s + 1, :], tail)
        out[s, BS : BS + TAIL] = mix.astype(jnp.int32).astype(jnp.int16)


def compact_kernel(pos, z, out, norm):
    p = pos[0]
    row = lax.broadcasted_iota(jnp.int32, (TAIL, BS), 0)
    tail = jnp.zeros((TAIL, BS), F32)
    for g in range(4):
        for blk in range(3):
            src = 4 * g + blk + (p <= blk).astype(jnp.int32)
            n = 3 * g + blk
            out[BS * n : BS * n + BS] = z[src, 0:BS]
            e = z[src, BS : BS + TAIL].astype(jnp.int32).astype(F32)[0:1]
            tail = jnp.where(row == n, e, tail)
    out[BS * BPO : BS * BPO + TAIL] = tail.astype(jnp.int32).astype(jnp.int16)
    total = jnp.zeros((1, BS), F32)
    for s in range(NZ):
        t = z[s, BS : BS + TAIL].astype(jnp.int32).astype(F32)
        part = t[2:3] * F32(1.0 / 16384.0) + t[3:4] * F32(1.0 / 16384.0**2)
        total += part * jnp.exp2(0.5 * t[1:2]) * jnp.exp2(0.5 * t[1:2])
    norm[...] = jnp.broadcast_to(total[None], norm.shape)


def update_kernel(code, tail, norm, clip, params, mom, tall, wide, new_p, new_m):
    i = pl.program_id(0)
    total = jnp.sum(jnp.sum(norm[...], axis=0), axis=1, keepdims=True)
    factor = jnp.minimum(F32(1.0), clip[0] * F32(math.sqrt(D * FF)) / (jnp.sqrt(total) + F32(EPSILON)))
    row = lax.broadcasted_iota(jnp.int32, (TAIL, BS), 0)
    exps = tail[...].astype(jnp.int32).astype(F32)
    for n in range(3):
        e = jnp.sum(jnp.where(row == 3 * i + n, exps, 0.0), axis=0, keepdims=True)
        d = slice(BS * n, BS * n + BS)
        coef = code[d].astype(jnp.int32).astype(F32) * (jnp.exp2(e - 15.0) * factor)
        upd = tall_times(tall[...], times_wide(coef, wide[...]))
        nm = NESTEROV * mom[d] + upd
        new_m[d] = nm
        new_p[d] = params[d] - OUTER_RATE * (upd + NESTEROV * nm)


SMEM = pl.BlockSpec(memory_space=pltpu.SMEM)
VMEM = pl.BlockSpec(memory_space=pltpu.VMEM)
BIG = pltpu.CompilerParams(vmem_limit_bytes=40 * 1024 * 1024)


def call(kernel, out_shape, inputs, name, scratch=()):
    return pl.pallas_call(
        kernel,
        out_shape=out_shape,
        in_specs=[SMEM if i.dtype == jnp.int32 else VMEM for i in inputs],
        out_specs=jax.tree.map(lambda _: VMEM, out_shape),
        scratch_shapes=scratch,
        compiler_params=BIG,
        name=name,
    )(*inputs)


def per_device(pseudo_grads, outer_params, momentum, clip_level, block_picks, cutoffs):
    z = lax.axis_index("z")
    pos = jnp.stack([z % 4, lax.axis_index("c"), z // 4]).astype(jnp.int32)
    hi, lo = table_parts()
    fwd_wide = jnp.asarray(np.concatenate([hi.T, lo.T], axis=1))
    fwd_tall = jnp.asarray(np.concatenate([hi, lo], axis=0))
    inv_wide = jnp.asarray(np.concatenate([hi, lo], axis=1))
    inv_tall = jnp.asarray(np.concatenate([hi.T, lo.T], axis=0))
    rows = pseudo_grads.shape[1]
    swap = [(NY * i + j, NX * j + i) for i in range(NX) for j in range(NY)]
    shape = jax.ShapeDtypeStruct

    picks, cuts = (
        lax.dynamic_index_in_dim(v[:, 0], lax.axis_index("x"), 1, keepdims=False) for v in (block_picks, cutoffs)
    )
    hit = picks[:, :, None] == jnp.arange(BPO, dtype=jnp.int32)
    cut = jnp.max(jnp.where(hit, cuts[:, :, None], -1), axis=1)
    cut = jnp.pad(cut.T.reshape(4, BPO), ((0, 4), (0, BS - BPO)))
    cut, pseudo_grads = lax.optimization_barrier((cut, pseudo_grads))
    near = []
    for n in range(4):
        near.append(
            lax.ppermute(
                cut,
                ("x", "y", "z"),
                [
                    ((NY * i + j) * NZ + 4 * g + q, (NX * j + i) * NZ + 4 * g + (q + n) % 4)
                    for i in range(NX)
                    for j in range(NY)
                    for g in range(4)
                    for q in range(4)
                ],
            )
        )
    near = jnp.stack(near)
    far = [near] + [lax.ppermute(near, "z", [(i, (i + 4 * n) % NZ) for i in range(NZ)]) for n in range(1, 4)]
    cut = lax.dynamic_index_in_dim(jnp.concatenate(far), z // 4, 1, keepdims=False)

    packed = pl.pallas_call(
        pack_kernel,
        out_shape=shape((NY, NC, NZ, rows, BS), BF16),
        grid=(NY,),
        in_specs=[SMEM, pl.BlockSpec((None, rows, FF // NY), lambda j: (0, 0, j))],
        out_specs=pl.BlockSpec((1, NC, NZ, rows, BS), lambda j: (j, 0, 0, 0, 0)),
        compiler_params=BIG,
        name="pack",
    )(pos, pseudo_grads)
    spread = lax.all_to_all(packed, "x", 0, 0, tiled=True)
    spread, cut = lax.optimization_barrier((spread, cut))
    other = lax.ppermute(spread[:, 1], "c", [(0, 1), (1, 0)])

    a, b = call(
        exchange_kernel,
        (shape((NX, 4, 96, BS), BF16), shape((NX, 8, 64, BS), BF16)),
        (pos, spread, other),
        "exchange",
    )
    pair_a, pair_b = [], []
    for g in range(0, NZ, 4):
        pair_a += [(g, g + 1), (g + 1, g), (g + 2, g + 3), (g + 3, g + 2)]
        pair_b += [(g + 1, g + 2), (g + 2, g + 1)]
    a = lax.ppermute(a, "z", pair_a)
    b = lax.ppermute(b, "z", pair_b)

    coded = call(
        forward_kernel,
        shape((NZ, BS + TAIL, BS), jnp.int16),
        (pos, cut, spread, other, a, b, fwd_tall, fwd_wide),
        "forward",
        [pltpu.VMEM((NX, BPO, BS, BS), BF16), pltpu.VMEM((NZ, BS), F32)],
    )
    coded = lax.all_to_all(coded, "z", 0, 0, tiled=True)
    coded, norm = call(
        compact_kernel,
        (shape((BPO * BS + TAIL, BS), jnp.int16), shape((NX * NY * NC, 1, BS), F32)),
        (pos, coded),
        "compact",
    )
    coded = lax.ppermute(coded, ("x", "y"), swap)
    norm = lax.all_to_all(norm, ("x", "y", "c"), 0, 0, tiled=True)

    tile = pl.BlockSpec((3 * BS, BS), lambda i: (i, 0))
    return pl.pallas_call(
        update_kernel,
        out_shape=(shape(outer_params.shape, F32), shape(outer_params.shape, F32)),
        grid=(4,),
        in_specs=[
            tile,
            pl.BlockSpec((TAIL, BS), lambda i: (BPO * BS // TAIL, 0)),
            VMEM,
            SMEM,
            tile,
            tile,
            VMEM,
            VMEM,
        ],
        out_specs=(tile, tile),
        compiler_params=BIG,
        name="update",
    )(coded, coded, norm, clip_level, outer_params, momentum, inv_tall, inv_wide)


def solution(mesh):
    grid = Mesh(mesh.devices.reshape(NX, NY, NZ, NC), ("x", "y", "z", "c"))
    yzc = ("y", "z", "c")
    in_specs = (P("x", yzc, None), P("x", yzc), P("x", yzc), P(), P(None, yzc, None, None), P(None, yzc, None, None))
    out_specs = (P("x", yzc), P("x", yzc))
    return jax.shard_map(per_device, mesh=grid, in_specs=in_specs, out_specs=out_specs, check_vma=False)
```

```python
import functools
import math

import jax
import jax.numpy as jnp
import ml_dtypes
import numpy as np
from jax import lax
from jax.experimental import pallas as pl
from jax.experimental.pallas import tpu as pltpu
from jax.sharding import Mesh, PartitionSpec as P

BS = 128
D = 6144
FF = 16384
OUTER_RATE = 0.7
NESTEROV = 0.9
EPSILON = 1e-06
NX, NY, NZ, NC = 4, 4, 16, 2
BPO = 12
TAIL = 16
F32 = jnp.float32
BF16 = jnp.bfloat16


def table_parts():
    u = np.arange(BS, dtype=np.float64)[:, None]
    k = np.arange(BS, dtype=np.float64)[None, :]
    c = np.cos(math.pi * (2.0 * k + 1.0) * u / (2.0 * BS)) * math.sqrt(2.0 / BS)
    c[0] *= math.sqrt(0.5)
    hi = c.astype(ml_dtypes.bfloat16)
    lo = (c - hi.astype(np.float64)).astype(ml_dtypes.bfloat16)
    return hi, lo


def dot(a, b):
    return lax.dot_general(a, b, (((1,), (0,)), ((), ())), preferred_element_type=F32)


def split(v):
    hi = v.astype(BF16)
    return hi, (v - hi.astype(F32)).astype(BF16)


def times_wide(v, wide):
    hi, lo = split(v)
    both = dot(hi, wide)
    return both[:, :BS] + both[:, BS:] + dot(lo, wide[:, :BS])


def tall_times(tall, v):
    hi, lo = split(v)
    both = dot(tall, hi)
    return both[:BS] + both[BS:] + dot(tall[:BS], lo)


def pack_kernel(pos, g, keep, give):
    c = pos[1]
    for out, core in ((keep, c), (give, 1 - c)):
        for m in range(4):
            for w in range(4):
                start = pl.multiple_of((2 * (4 * w + m) + core) * BS, BS)
                out[0, 4 * m + w] = g[:, pl.ds(start, BS)]


def by_place(pos, spread, body):
    mine, other = spread.at[:, 0], spread.at[:, 1]
    for p in range(4):
        for c in range(2):

            @pl.when((pos[0] == p) & (pos[1] == c))
            def _(p=p, c=c):
                if c == 0:
                    body(p, mine, other)
                else:
                    body(p, other, mine)


def exchange_kernel(pos, spread, a, b):
    def body(p, lo, hi):
        if p in (0, 3):
            s = slice(0, 4) if p == 0 else slice(12, 16)
            a[:, :, 0:48] = lo[:, s]
            a[:, :, 48:96] = hi[:, s]
            return
        for k in range(3):
            if p == 1:
                a[:, :, 32 * k : 32 * k + 32] = lo[:, 4 * k + 4 : 4 * k + 8, 0:32]
            else:
                a[:, :, 32 * k : 32 * k + 32] = hi[:, 4 * k : 4 * k + 4, 16:48]
        if p == 1:
            b[:, :, 0:16] = lo[:, 0:8, 32:48]
            b[:, :, 16:64] = hi[:, 0:8]
        else:
            b[:, :, 0:48] = lo[:, 8:16]
            b[:, :, 48:64] = hi[:, 8:16, 0:16]

    by_place(pos, spread, body)


def assemble(pos, spread, a, b, whole):
    def place(p, k, lo, hi, x):
        m = k + (k >= p)
        s = slice(4 * m, 4 * m + 4)
        third = slice(32 * k, 32 * k + 32)
        if p == 0:
            x[:, :, 0:48] = lo[:, s]
            x[:, :, 48:96] = hi[:, s]
            x[:, :, 96:128] = a[:, :, third]
        elif p == 3:
            x[:, :, 0:32] = a[:, :, third]
            x[:, :, 32:80] = lo[:, s]
            x[:, :, 80:128] = hi[:, s]
        elif p == 1 and m == 0:
            x[:, :, 0:96] = a[:, :, :]
            x[:, :, 96:128] = lo[:, s, 0:32]
        elif p == 1:
            x[:, :, 0:16] = lo[:, s, 32:48]
            x[:, :, 16:64] = hi[:, s]
            x[:, :, 64:128] = b[:, 4 * (m - 2) : 4 * (m - 2) + 4]
        elif m == 3:
            x[:, :, 0:32] = hi[:, s, 16:48]
            x[:, :, 32:128] = a[:, :, :]
        else:
            x[:, :, 0:64] = b[:, s]
            x[:, :, 64:112] = lo[:, s]
            x[:, :, 112:128] = hi[:, s, 0:16]

    def body(p, lo, hi):
        for k in range(3):
            place(p, k, lo, hi, whole.at[:, 4 * k : 4 * k + 4])

    by_place(pos, spread, body)


def exponent(size):
    return jnp.clip(jnp.floor(jnp.log2(jnp.maximum(size, F32(1e-30)))) + 1.0, -100.0, 200.0)


def forward_kernel(pos, cut, spread, a, b, left, wide, out, x, exps):
    assemble(pos, spread, a, b, x)
    p = pos[0]
    freq = lax.broadcasted_iota(jnp.int32, (BS, BS), 0) + lax.broadcasted_iota(jnp.int32, (BS, BS), 1)
    row = lax.broadcasted_iota(jnp.int32, (TAIL, BS), 0)
    exps[...] = jnp.zeros_like(exps)
    for w in range(4):
        out[4 * w + p, 0:BS] = jnp.zeros((BS, BS), jnp.int16)

    def step(w, square):
        for k in range(3):
            m = k + (k >= p).astype(jnp.int32)
            blk = p - (p > m).astype(jnp.int32)
            total = jnp.zeros((BS, BS), F32)
            for r in range(NX):
                both = dot(x[r, 4 * k + w], wide[...])
                hi, lo = split(both[:, :BS] + both[:, BS:])
                pairs = jnp.concatenate(
                    [
                        jnp.concatenate([hi, lo], axis=1),
                        jnp.concatenate([hi, jnp.zeros_like(lo)], axis=1),
                    ],
                    axis=0,
                )
                both = dot(left[...], pairs)
                coef = both[:, :BS] + both[:, BS:]
                total += jnp.where(freq <= cut[4 * w + m, 4 * blk + r], coef, 0.0)
            e = exponent(jnp.max(jnp.abs(total), axis=0, keepdims=True))
            code = jnp.clip(jnp.floor(total * jnp.exp2(15.0 - e) + 0.5), -32767.0, 32767.0)
            out[4 * w + m, 0:BS] = code.astype(jnp.int32).astype(jnp.int16)
            exps[pl.ds(4 * w + m, 1), :] = e
            square += jnp.sum(total * total, axis=0, keepdims=True)
        return square

    square = jnp.zeros((1, BS), F32)
    for w in range(4):
        square = step(w, square)
    e = exponent(square)
    scaled = jnp.minimum(square, F32(3e38)) * jnp.exp2(-0.5 * e) * jnp.exp2(-0.5 * e) * 16384.0
    d1 = jnp.floor(scaled)
    d2 = jnp.floor((scaled - d1) * 16384.0)
    e = jnp.where(square > F32(3e38), 200.0, e)
    tail = jnp.where(row == 1, e, jnp.where(row == 2, d1, jnp.where(row == 3, d2, 0.0)))
    for s in range(NZ):
        mix = jnp.where(row == 0, exps[s : s + 1, :], tail)
        out[s, BS : BS + TAIL] = mix.astype(jnp.int32).astype(jnp.int16)


def compact_kernel(pos, z, out, norm):
    p = pos[0]
    row = lax.broadcasted_iota(jnp.int32, (TAIL, BS), 0)
    tail = jnp.zeros((TAIL, BS), F32)
    for g in range(4):
        for blk in range(3):
            src = 4 * g + blk + (p <= blk).astype(jnp.int32)
            n = 3 * g + blk
            out[BS * n : BS * n + BS] = z[src, 0:BS]
            e = z[src, BS : BS + TAIL].astype(jnp.int32).astype(F32)[0:1]
            tail = jnp.where(row == n, e, tail)
    out[BS * BPO : BS * BPO + TAIL] = tail.astype(jnp.int32).astype(jnp.int16)
    total = jnp.zeros((1, BS), F32)
    for s in range(NZ):
        t = z[s, BS : BS + TAIL].astype(jnp.int32).astype(F32)
        part = t[2:3] * F32(1.0 / 16384.0) + t[3:4] * F32(1.0 / 16384.0**2)
        total += part * jnp.exp2(0.5 * t[1:2]) * jnp.exp2(0.5 * t[1:2])
    norm[...] = jnp.broadcast_to(total[None], norm.shape)


def update_kernel(code, tail, norm, clip, params, mom, tall, wide, new_p, new_m):
    i = pl.program_id(0)
    total = jnp.sum(jnp.sum(norm[...], axis=0), axis=1, keepdims=True)
    factor = jnp.minimum(F32(1.0), clip[0] * F32(math.sqrt(D * FF)) / (jnp.sqrt(total) + F32(EPSILON)))
    row = lax.broadcasted_iota(jnp.int32, (TAIL, BS), 0)
    exps = tail[...].astype(jnp.int32).astype(F32)
    for n in range(3):
        e = jnp.sum(jnp.where(row == 3 * i + n, exps, 0.0), axis=0, keepdims=True)
        d = slice(BS * n, BS * n + BS)
        coef = code[d].astype(jnp.int32).astype(F32) * (jnp.exp2(e - 15.0) * factor)
        upd = tall_times(tall[...], times_wide(coef, wide[...]))
        nm = NESTEROV * mom[d] + upd
        new_m[d] = nm
        new_p[d] = params[d] - OUTER_RATE * (upd + NESTEROV * nm)


SMEM = pl.BlockSpec(memory_space=pltpu.SMEM)
VMEM = pl.BlockSpec(memory_space=pltpu.VMEM)
BIG = pltpu.CompilerParams(vmem_limit_bytes=40 * 1024 * 1024)


def call(kernel, out_shape, inputs, name, scratch=()):
    return pl.pallas_call(
        kernel,
        out_shape=out_shape,
        in_specs=[SMEM if i.dtype == jnp.int32 else VMEM for i in inputs],
        out_specs=jax.tree.map(lambda _: VMEM, out_shape),
        scratch_shapes=scratch,
        compiler_params=BIG,
        name=name,
    )(*inputs)


def per_device(pseudo_grads, outer_params, momentum, clip_level, block_picks, cutoffs):
    z = lax.axis_index("z")
    pos = jnp.stack([z % 4, lax.axis_index("c")]).astype(jnp.int32)
    hi, lo = table_parts()
    fwd_wide = jnp.asarray(np.concatenate([hi.T, lo.T], axis=1))
    inv_wide = jnp.asarray(np.concatenate([hi, lo], axis=1))
    inv_tall = jnp.asarray(np.concatenate([hi.T, lo.T], axis=0))
    rows = pseudo_grads.shape[1]
    swap = [(NY * i + j, NX * j + i) for i in range(NX) for j in range(NY)]
    shape = jax.ShapeDtypeStruct

    hit = block_picks[:, 0, :, :, None] == jnp.arange(BPO, dtype=jnp.int32)
    cut = jnp.max(jnp.where(hit, cutoffs[:, 0, :, :, None], -1), axis=2)
    cut = cut.transpose(1, 2, 0).reshape(NY, 4, 1, BPO)
    cut = jnp.broadcast_to(cut, (NY, 4, 4, BPO)).reshape(NY * NZ, 1, BPO)
    cut = jnp.pad(cut, ((0, 0), (0, 0), (0, BS - BPO)))
    cut = lax.all_to_all(cut, ("y", "z"), 0, 0, tiled=True)
    cut = lax.dynamic_slice_in_dim(cut[:, 0], lax.axis_index("x") * NZ, NZ, 0)

    part = pl.BlockSpec((1, NZ, rows, BS), lambda j: (j, 0, 0, 0))
    keep, give = pl.pallas_call(
        pack_kernel,
        out_shape=[shape((NY, NZ, rows, BS), BF16)] * 2,
        grid=(NY,),
        in_specs=[SMEM, pl.BlockSpec((None, rows, FF // NY), lambda j: (0, 0, j))],
        out_specs=[part, part],
        compiler_params=BIG,
        name="pack",
    )(pos, pseudo_grads)
    got = lax.ppermute(give, "c", [(0, 1), (1, 0)])
    chip = jnp.stack([keep, got], axis=1)
    chip, cut = lax.optimization_barrier((chip, cut))
    spread = lax.all_to_all(chip, "x", 0, 0, tiled=True)

    a, b = call(
        exchange_kernel,
        (shape((NX, 4, 96, BS), BF16), shape((NX, 8, 64, BS), BF16)),
        (pos, spread),
        "exchange",
    )
    pair_a, pair_b = [], []
    for g in range(0, NZ, 4):
        pair_a += [(g, g + 1), (g + 1, g), (g + 2, g + 3), (g + 3, g + 2)]
        pair_b += [(g + 1, g + 2), (g + 2, g + 1)]
    a = lax.ppermute(a, "z", pair_a)
    b = lax.ppermute(b, "z", pair_b)

    coded = call(
        forward_kernel,
        shape((NZ, BS + TAIL, BS), jnp.int16),
        (pos, cut, spread, a, b, inv_wide, fwd_wide),
        "forward",
        [pltpu.VMEM((NX, BPO, BS, BS), BF16), pltpu.VMEM((NZ, BS), F32)],
    )
    coded = lax.all_to_all(coded, "z", 0, 0, tiled=True)
    coded, norm = call(
        compact_kernel,
        (shape((BPO * BS + TAIL, BS), jnp.int16), shape((NX * NY * NC, 1, BS), F32)),
        (pos, coded),
        "compact",
    )
    coded = lax.ppermute(coded, ("x", "y"), swap)
    norm = lax.all_to_all(norm, ("x", "y", "c"), 0, 0, tiled=True)

    tile = pl.BlockSpec((3 * BS, BS), lambda i: (i, 0))
    return pl.pallas_call(
        update_kernel,
        out_shape=(shape(outer_params.shape, F32), shape(outer_params.shape, F32)),
        grid=(4,),
        in_specs=[
            tile,
            pl.BlockSpec((TAIL, BS), lambda i: (BPO * BS // TAIL, 0)),
            VMEM,
            SMEM,
            tile,
            tile,
            VMEM,
            VMEM,
        ],
        out_specs=(tile, tile),
        compiler_params=BIG,
        name="update",
    )(coded, coded, norm, clip_level, outer_params, momentum, inv_tall, inv_wide)


def solution(mesh):
    grid = Mesh(mesh.devices.reshape(NX, NY, NZ, NC), ("x", "y", "z", "c"))
    yzc = ("y", "z", "c")
    in_specs = (P("x", yzc, None), P("x", yzc), P("x", yzc), P(), P(None, yzc, None, None), P(None, yzc, None, None))
    out_specs = (P("x", yzc), P("x", yzc))
    return jax.shard_map(per_device, mesh=grid, in_specs=in_specs, out_specs=out_specs, check_vma=False)
```

```python
import functools
import math

import jax
import jax.numpy as jnp
import ml_dtypes
import numpy as np
from jax import lax
from jax.experimental import pallas as pl
from jax.experimental.pallas import tpu as pltpu
from jax.sharding import Mesh, PartitionSpec as P

BS = 128
D = 6144
FF = 16384
OUTER_RATE = 0.7
NESTEROV = 0.9
EPSILON = 1e-06
NX, NY, NZ, NC = 4, 4, 16, 2
BPO = 12
TAIL = 16
F32 = jnp.float32
BF16 = jnp.bfloat16


def table_parts():
    u = np.arange(BS, dtype=np.float64)[:, None]
    k = np.arange(BS, dtype=np.float64)[None, :]
    c = np.cos(math.pi * (2.0 * k + 1.0) * u / (2.0 * BS)) * math.sqrt(2.0 / BS)
    c[0] *= math.sqrt(0.5)
    hi = c.astype(ml_dtypes.bfloat16)
    lo = (c - hi.astype(np.float64)).astype(ml_dtypes.bfloat16)
    return hi, lo


def dot(a, b):
    return lax.dot_general(a, b, (((1,), (0,)), ((), ())), preferred_element_type=F32)


def split(v):
    hi = v.astype(BF16)
    return hi, (v - hi.astype(F32)).astype(BF16)


def times_wide(v, wide):
    hi, lo = split(v)
    both = dot(hi, wide)
    return both[:, :BS] + both[:, BS:] + dot(lo, wide[:, :BS])


def tall_times(tall, v):
    hi, lo = split(v)
    both = dot(tall, hi)
    return both[:BS] + both[BS:] + dot(tall[:BS], lo)


def pack_kernel(g, out):
    for core in range(NC):
        for m in range(4):
            for w in range(4):
                start = (2 * (4 * w + m) + core) * BS
                out[0, core, 4 * m + w] = g[:, start : start + BS]


def by_place(pos, spread, body):
    for p in range(4):
        pl.when(pos[0] == p)(functools.partial(body, p, spread.at[:, 0], spread.at[:, 1]))


def exchange_kernel(pos, spread, a, b):
    def body(p, lo, hi):
        if p in (0, 3):
            s = slice(0, 4) if p == 0 else slice(12, 16)
            a[:, :, 0:48] = lo[:, s]
            a[:, :, 48:96] = hi[:, s]
            return
        for k in range(3):
            if p == 1:
                a[:, :, 32 * k : 32 * k + 32] = lo[:, 4 * k + 4 : 4 * k + 8, 0:32]
            else:
                a[:, :, 32 * k : 32 * k + 32] = hi[:, 4 * k : 4 * k + 4, 16:48]
        if p == 1:
            b[:, :, 0:16] = lo[:, 0:8, 32:48]
            b[:, :, 16:64] = hi[:, 0:8]
        else:
            b[:, :, 0:48] = lo[:, 8:16]
            b[:, :, 48:64] = hi[:, 8:16, 0:16]

    by_place(pos, spread, body)


def assemble(pos, spread, a, b, whole):
    def place(p, k, lo, hi, x):
        m = k + (k >= p)
        s = slice(4 * m, 4 * m + 4)
        third = slice(32 * k, 32 * k + 32)
        if p == 0:
            x[:, :, 0:48] = lo[:, s]
            x[:, :, 48:96] = hi[:, s]
            x[:, :, 96:128] = a[:, :, third]
        elif p == 3:
            x[:, :, 0:32] = a[:, :, third]
            x[:, :, 32:80] = lo[:, s]
            x[:, :, 80:128] = hi[:, s]
        elif p == 1 and m == 0:
            x[:, :, 0:96] = a[:, :, :]
            x[:, :, 96:128] = lo[:, s, 0:32]
        elif p == 1:
            x[:, :, 0:16] = lo[:, s, 32:48]
            x[:, :, 16:64] = hi[:, s]
            x[:, :, 64:128] = b[:, 4 * (m - 2) : 4 * (m - 2) + 4]
        elif m == 3:
            x[:, :, 0:32] = hi[:, s, 16:48]
            x[:, :, 32:128] = a[:, :, :]
        else:
            x[:, :, 0:64] = b[:, s]
            x[:, :, 64:112] = lo[:, s]
            x[:, :, 112:128] = hi[:, s, 0:16]

    def body(p, lo, hi):
        for k in range(3):
            place(p, k, lo, hi, whole.at[:, 4 * k : 4 * k + 4])

    by_place(pos, spread, body)


def exponent(size):
    return jnp.clip(jnp.floor(jnp.log2(jnp.maximum(size, F32(1e-30)))) + 1.0, -100.0, 200.0)


def forward_kernel(pos, spread, a, b, left, wide, out, x):
    assemble(pos, spread, a, b, x)
    for i in range(BPO):
        for r in range(NX):
            both = dot(x[r, i], wide[...])
            hi, lo = split(both[:, :BS] + both[:, BS:])
            pairs = jnp.concatenate(
                [
                    jnp.concatenate([hi, lo], axis=1),
                    jnp.concatenate([hi, jnp.zeros_like(lo)], axis=1),
                ],
                axis=0,
            )
            both = dot(left[...], pairs)
            out[i, r] = both[:, :BS] + both[:, BS:]


def mask_kernel(pos, cut, coef, out, exps):
    p = pos[0]
    freq = lax.broadcasted_iota(jnp.int32, (BS, BS), 0) + lax.broadcasted_iota(jnp.int32, (BS, BS), 1)
    row = lax.broadcasted_iota(jnp.int32, (TAIL, BS), 0)
    exps[...] = jnp.zeros_like(exps)
    for w in range(4):
        out[4 * w + p, 0:BS] = jnp.zeros((BS, BS), jnp.int16)
    square = jnp.zeros((1, BS), F32)
    for i in range(BPO):
        k, w = divmod(i, 4)
        m = k + (k >= p).astype(jnp.int32)
        blk = p - (p > m).astype(jnp.int32)
        total = jnp.zeros((BS, BS), F32)
        for r in range(NX):
            total += jnp.where(freq <= cut[4 * w + m, 4 * blk + r], coef[i, r], 0.0)
        e = exponent(jnp.max(jnp.abs(total), axis=0, keepdims=True))
        code = jnp.clip(jnp.floor(total * jnp.exp2(15.0 - e) + 0.5), -32767.0, 32767.0)
        out[4 * w + m, 0:BS] = code.astype(jnp.int32).astype(jnp.int16)
        exps[pl.ds(4 * w + m, 1), :] = e
        square += jnp.sum(total * total, axis=0, keepdims=True)
    e = exponent(square)
    scaled = jnp.minimum(square, F32(3e38)) * jnp.exp2(-0.5 * e) * jnp.exp2(-0.5 * e) * 16384.0
    d1 = jnp.floor(scaled)
    d2 = jnp.floor((scaled - d1) * 16384.0)
    e = jnp.where(square > F32(3e38), 200.0, e)
    tail = jnp.where(row == 1, e, jnp.where(row == 2, d1, jnp.where(row == 3, d2, 0.0)))
    for s in range(NZ):
        mix = jnp.where(row == 0, exps[s : s + 1, :], tail)
        out[s, BS : BS + TAIL] = mix.astype(jnp.int32).astype(jnp.int16)


def compact_kernel(pos, z, out, norm):
    p = pos[0]
    row = lax.broadcasted_iota(jnp.int32, (TAIL, BS), 0)
    tail = jnp.zeros((TAIL, BS), F32)
    for g in range(4):
        for blk in range(3):
            src = 4 * g + blk + (p <= blk).astype(jnp.int32)
            n = 3 * g + blk
            out[BS * n : BS * n + BS] = z[src, 0:BS]
            e = z[src, BS : BS + TAIL].astype(jnp.int32).astype(F32)[0:1]
            tail = jnp.where(row == n, e, tail)
    out[BS * BPO : BS * BPO + TAIL] = tail.astype(jnp.int32).astype(jnp.int16)
    total = jnp.zeros((1, BS), F32)
    for s in range(NZ):
        t = z[s, BS : BS + TAIL].astype(jnp.int32).astype(F32)
        part = t[2:3] * F32(1.0 / 16384.0) + t[3:4] * F32(1.0 / 16384.0**2)
        total += part * jnp.exp2(0.5 * t[1:2]) * jnp.exp2(0.5 * t[1:2])
    norm[...] = jnp.broadcast_to(total[None], norm.shape)


def update_kernel(code, tail, norm, clip, params, mom, tall, wide, new_p, new_m):
    i = pl.program_id(0)
    total = jnp.sum(jnp.sum(norm[...], axis=0), axis=1, keepdims=True)
    factor = jnp.minimum(F32(1.0), clip[0] * F32(math.sqrt(D * FF)) / (jnp.sqrt(total) + F32(EPSILON)))
    row = lax.broadcasted_iota(jnp.int32, (TAIL, BS), 0)
    exps = tail[...].astype(jnp.int32).astype(F32)
    for n in range(3):
        e = jnp.sum(jnp.where(row == 3 * i + n, exps, 0.0), axis=0, keepdims=True)
        d = slice(BS * n, BS * n + BS)
        coef = code[d].astype(jnp.int32).astype(F32) * (jnp.exp2(e - 15.0) * factor)
        upd = tall_times(tall[...], times_wide(coef, wide[...]))
        nm = NESTEROV * mom[d] + upd
        new_m[d] = nm
        new_p[d] = params[d] - OUTER_RATE * (upd + NESTEROV * nm)


SMEM = pl.BlockSpec(memory_space=pltpu.SMEM)
VMEM = pl.BlockSpec(memory_space=pltpu.VMEM)
BIG = pltpu.CompilerParams(vmem_limit_bytes=16 * 1024 * 1024)


def call(kernel, out_shape, inputs, name, scratch=()):
    return pl.pallas_call(
        kernel,
        out_shape=out_shape,
        in_specs=[SMEM if i.dtype == jnp.int32 else VMEM for i in inputs],
        out_specs=jax.tree.map(lambda _: VMEM, out_shape),
        scratch_shapes=scratch,
        compiler_params=BIG,
        name=name,
    )(*inputs)


def per_device(pseudo_grads, outer_params, momentum, clip_level, block_picks, cutoffs):
    z = lax.axis_index("z")
    pos = (z % 4).astype(jnp.int32).reshape(1)
    hi, lo = table_parts()
    fwd_wide = jnp.asarray(np.concatenate([hi.T, lo.T], axis=1))
    inv_wide = jnp.asarray(np.concatenate([hi, lo], axis=1))
    inv_tall = jnp.asarray(np.concatenate([hi.T, lo.T], axis=0))
    rows = pseudo_grads.shape[1]
    swap = [(NY * i + j, NX * j + i) for i in range(NX) for j in range(NY)]
    shape = jax.ShapeDtypeStruct

    picks, cuts = (
        lax.dynamic_index_in_dim(v[:, 0], lax.axis_index("x"), 1, keepdims=False) for v in (block_picks, cutoffs)
    )
    hit = picks[:, :, None] == jnp.arange(BPO, dtype=jnp.int32)
    cut = jnp.max(jnp.where(hit, cuts[:, :, None], -1), axis=1)
    cut = jnp.pad(cut.T.reshape(4, BPO), ((0, 4), (0, BS - BPO)))
    cut, pseudo_grads = lax.optimization_barrier((cut, pseudo_grads))
    cut = lax.ppermute(cut, ("x", "y"), swap)

    chip = pl.pallas_call(
        pack_kernel,
        out_shape=shape((NY, NC, NZ, rows, BS), BF16),
        grid=(NY,),
        in_specs=[pl.BlockSpec((None, rows, FF // NY), lambda j: (0, 0, j))],
        out_specs=pl.BlockSpec((1, NC, NZ, rows, BS), lambda j: (j, 0, 0, 0, 0)),
        compiler_params=BIG,
        name="pack",
    )(pseudo_grads)
    chip = lax.all_to_all(chip.reshape(NY * NC, NZ, rows, BS), ("x", "c"), 0, 0, tiled=True)
    spread = chip.reshape(NX, NC, NZ, rows, BS)
    spread, cut = lax.optimization_barrier((spread, cut))

    a, b = call(
        exchange_kernel,
        (shape((NX, 4, 96, BS), BF16), shape((NX, 8, 64, BS), BF16)),
        (pos, spread),
        "exchange",
    )
    pair_a, pair_b = [], []
    for g in range(0, NZ, 4):
        pair_a += [(g, g + 1), (g + 1, g), (g + 2, g + 3), (g + 3, g + 2)]
        pair_b += [(g + 1, g + 2), (g + 2, g + 1)]
    a = lax.ppermute(a, "z", pair_a)
    b = lax.ppermute(b, "z", pair_b)

    cut = jnp.broadcast_to(cut[:4, None], (4, 4, BS)).reshape(NZ, 1, BS)
    cut, a, b = lax.optimization_barrier((cut, a, b))
    cut = lax.all_to_all(cut, "z", 0, 0, tiled=True)[:, 0]

    coef = call(
        forward_kernel,
        shape((BPO, NX, BS, BS), F32),
        (pos, spread, a, b, inv_wide, fwd_wide),
        "forward",
        [pltpu.VMEM((NX, BPO, BS, BS), BF16)],
    )
    coded = call(
        mask_kernel,
        shape((NZ, BS + TAIL, BS), jnp.int16),
        (pos, cut, coef),
        "mask",
        [pltpu.VMEM((NZ, BS), F32)],
    )
    coded = lax.all_to_all(coded, "z", 0, 0, tiled=True)
    coded, norm = call(
        compact_kernel,
        (shape((BPO * BS + TAIL, BS), jnp.int16), shape((NX * NY * NC, 1, BS), F32)),
        (pos, coded),
        "compact",
    )
    coded = lax.ppermute(coded, ("x", "y"), swap)
    norm = lax.all_to_all(norm, ("x", "y", "c"), 0, 0, tiled=True)

    tile = pl.BlockSpec((3 * BS, BS), lambda i: (i, 0))
    return pl.pallas_call(
        update_kernel,
        out_shape=(shape(outer_params.shape, F32), shape(outer_params.shape, F32)),
        grid=(4,),
        in_specs=[
            tile,
            pl.BlockSpec((TAIL, BS), lambda i: (BPO * BS // TAIL, 0)),
            VMEM,
            SMEM,
            tile,
            tile,
            VMEM,
            VMEM,
        ],
        out_specs=(tile, tile),
        compiler_params=BIG,
        name="update",
    )(coded, coded, norm, clip_level, outer_params, momentum, inv_tall, inv_wide)


def solution(mesh):
    grid = Mesh(mesh.devices.reshape(NX, NY, NZ, NC), ("x", "y", "z", "c"))
    yzc = ("y", "z", "c")
    in_specs = (P("x", yzc, None), P("x", yzc), P("x", yzc), P(), P(None, yzc, None, None), P(None, yzc, None, None))
    out_specs = (P("x", yzc), P("x", yzc))
    return jax.shard_map(per_device, mesh=grid, in_specs=in_specs, out_specs=out_specs, check_vma=False)
```

```python
import functools
import math

import jax
import jax.numpy as jnp
import ml_dtypes
import numpy as np
from jax import lax
from jax.experimental import pallas as pl
from jax.experimental.pallas import tpu as pltpu
from jax.sharding import Mesh, PartitionSpec as P

BS = 128
D = 6144
FF = 16384
OUTER_RATE = 0.7
NESTEROV = 0.9
EPSILON = 1e-06
NX, NY, NZ, NC = 4, 4, 16, 2
BPO = 12
TAIL = 16
F32 = jnp.float32
BF16 = jnp.bfloat16


def table_parts():
    u = np.arange(BS, dtype=np.float64)[:, None]
    k = np.arange(BS, dtype=np.float64)[None, :]
    c = np.cos(math.pi * (2.0 * k + 1.0) * u / (2.0 * BS)) * math.sqrt(2.0 / BS)
    c[0] *= math.sqrt(0.5)
    hi = c.astype(ml_dtypes.bfloat16)
    lo = (c - hi.astype(np.float64)).astype(ml_dtypes.bfloat16)
    return hi, lo


def dot(a, b):
    return lax.dot_general(a, b, (((1,), (0,)), ((), ())), preferred_element_type=F32)


def split(v):
    hi = v.astype(BF16)
    return hi, (v - hi.astype(F32)).astype(BF16)


def times_wide(v, wide):
    hi, lo = split(v)
    both = dot(hi, wide)
    return both[:, :BS] + both[:, BS:] + dot(lo, wide[:, :BS])


def tall_times(tall, v):
    hi, lo = split(v)
    both = dot(tall, hi)
    return both[:BS] + both[BS:] + dot(tall[:BS], lo)


def pack_kernel(g, out):
    for core in range(NC):
        for m in range(4):
            for w in range(4):
                start = (2 * (4 * w + m) + core) * BS
                out[0, core, 4 * m + w] = g[:, start : start + BS]


def by_place(pos, spread, body):
    for p in range(4):
        pl.when(pos[0] == p)(functools.partial(body, p, spread.at[:, 0], spread.at[:, 1]))


def exchange_kernel(pos, spread, a, b):
    def body(p, lo, hi):
        if p in (0, 3):
            s = slice(0, 4) if p == 0 else slice(12, 16)
            a[:, :, 0:48] = lo[:, s]
            a[:, :, 48:96] = hi[:, s]
            return
        for k in range(3):
            if p == 1:
                a[:, :, 32 * k : 32 * k + 32] = lo[:, 4 * k + 4 : 4 * k + 8, 0:32]
            else:
                a[:, :, 32 * k : 32 * k + 32] = hi[:, 4 * k : 4 * k + 4, 16:48]
        if p == 1:
            b[:, :, 0:16] = lo[:, 0:8, 32:48]
            b[:, :, 16:64] = hi[:, 0:8]
        else:
            b[:, :, 0:48] = lo[:, 8:16]
            b[:, :, 48:64] = hi[:, 8:16, 0:16]

    by_place(pos, spread, body)


def assemble(pos, spread, a, b, whole):
    def place(p, k, lo, hi, x):
        m = k + (k >= p)
        s = slice(4 * m, 4 * m + 4)
        third = slice(32 * k, 32 * k + 32)
        if p == 0:
            x[:, :, 0:48] = lo[:, s]
            x[:, :, 48:96] = hi[:, s]
            x[:, :, 96:128] = a[:, :, third]
        elif p == 3:
            x[:, :, 0:32] = a[:, :, third]
            x[:, :, 32:80] = lo[:, s]
            x[:, :, 80:128] = hi[:, s]
        elif p == 1 and m == 0:
            x[:, :, 0:96] = a[:, :, :]
            x[:, :, 96:128] = lo[:, s, 0:32]
        elif p == 1:
            x[:, :, 0:16] = lo[:, s, 32:48]
            x[:, :, 16:64] = hi[:, s]
            x[:, :, 64:128] = b[:, 4 * (m - 2) : 4 * (m - 2) + 4]
        elif m == 3:
            x[:, :, 0:32] = hi[:, s, 16:48]
            x[:, :, 32:128] = a[:, :, :]
        else:
            x[:, :, 0:64] = b[:, s]
            x[:, :, 64:112] = lo[:, s]
            x[:, :, 112:128] = hi[:, s, 0:16]

    def body(p, lo, hi):
        for k in range(3):
            place(p, k, lo, hi, whole.at[:, 4 * k : 4 * k + 4])

    by_place(pos, spread, body)


def exponent(size):
    return jnp.clip(jnp.floor(jnp.log2(jnp.maximum(size, F32(1e-30)))) + 1.0, -100.0, 200.0)


def forward_kernel(pos, cut, spread, a, b, left, wide, out, x, exps):
    assemble(pos, spread, a, b, x)
    p = pos[0]
    freq = lax.broadcasted_iota(jnp.int32, (BS, BS), 0) + lax.broadcasted_iota(jnp.int32, (BS, BS), 1)
    row = lax.broadcasted_iota(jnp.int32, (TAIL, BS), 0)
    exps[...] = jnp.zeros_like(exps)
    for w in range(4):
        out[4 * w + p, 0:BS] = jnp.zeros((BS, BS), jnp.int16)

    def step(w, square):
        for k in range(3):
            m = k + (k >= p).astype(jnp.int32)
            blk = p - (p > m).astype(jnp.int32)
            total = jnp.zeros((BS, BS), F32)
            for r in range(NX):
                both = dot(x[r, 4 * k + w], wide[...])
                hi, lo = split(both[:, :BS] + both[:, BS:])
                pairs = jnp.concatenate(
                    [
                        jnp.concatenate([hi, lo], axis=1),
                        jnp.concatenate([hi, jnp.zeros_like(lo)], axis=1),
                    ],
                    axis=0,
                )
                both = dot(left[...], pairs)
                coef = both[:, :BS] + both[:, BS:]
                total += jnp.where(freq <= cut[4 * w + m, 4 * blk + r], coef, 0.0)
            e = exponent(jnp.max(jnp.abs(total), axis=0, keepdims=True))
            code = jnp.clip(jnp.floor(total * jnp.exp2(15.0 - e) + 0.5), -32767.0, 32767.0)
            out[4 * w + m, 0:BS] = code.astype(jnp.int32).astype(jnp.int16)
            exps[pl.ds(4 * w + m, 1), :] = e
            square += jnp.sum(total * total, axis=0, keepdims=True)
        return square

    square = jnp.zeros((1, BS), F32)
    for w in range(4):
        square = step(w, square)
    e = exponent(square)
    scaled = jnp.minimum(square, F32(3e38)) * jnp.exp2(-0.5 * e) * jnp.exp2(-0.5 * e) * 16384.0
    d1 = jnp.floor(scaled)
    d2 = jnp.floor((scaled - d1) * 16384.0)
    e = jnp.where(square > F32(3e38), 200.0, e)
    tail = jnp.where(row == 1, e, jnp.where(row == 2, d1, jnp.where(row == 3, d2, 0.0)))
    for s in range(NZ):
        mix = jnp.where(row == 0, exps[s : s + 1, :], tail)
        out[s, BS : BS + TAIL] = mix.astype(jnp.int32).astype(jnp.int16)


def compact_kernel(pos, z, out, norm):
    p = pos[0]
    row = lax.broadcasted_iota(jnp.int32, (TAIL, BS), 0)
    tail = jnp.zeros((TAIL, BS), F32)
    for g in range(4):
        for blk in range(3):
            src = 4 * g + blk + (p <= blk).astype(jnp.int32)
            n = 3 * g + blk
            out[BS * n : BS * n + BS] = z[src, 0:BS]
            e = z[src, BS : BS + TAIL].astype(jnp.int32).astype(F32)[0:1]
            tail = jnp.where(row == n, e, tail)
    out[BS * BPO : BS * BPO + TAIL] = tail.astype(jnp.int32).astype(jnp.int16)
    total = jnp.zeros((1, BS), F32)
    for s in range(NZ):
        t = z[s, BS : BS + TAIL].astype(jnp.int32).astype(F32)
        part = t[2:3] * F32(1.0 / 16384.0) + t[3:4] * F32(1.0 / 16384.0**2)
        total += part * jnp.exp2(0.5 * t[1:2]) * jnp.exp2(0.5 * t[1:2])
    norm[...] = jnp.broadcast_to(total[None], norm.shape)


def update_kernel(code, tail, norm, clip, params, mom, tall, wide, new_p, new_m):
    i = pl.program_id(0)
    total = jnp.sum(jnp.sum(norm[...], axis=0), axis=1, keepdims=True)
    factor = jnp.minimum(F32(1.0), clip[0] * F32(math.sqrt(D * FF)) / (jnp.sqrt(total) + F32(EPSILON)))
    row = lax.broadcasted_iota(jnp.int32, (TAIL, BS), 0)
    exps = tail[...].astype(jnp.int32).astype(F32)
    for n in range(3):
        e = jnp.sum(jnp.where(row == 3 * i + n, exps, 0.0), axis=0, keepdims=True)
        d = slice(BS * n, BS * n + BS)
        coef = code[d].astype(jnp.int32).astype(F32) * (jnp.exp2(e - 15.0) * factor)
        upd = tall_times(tall[...], times_wide(coef, wide[...]))
        nm = NESTEROV * mom[d] + upd
        new_m[d] = nm
        new_p[d] = params[d] - OUTER_RATE * (upd + NESTEROV * nm)


SMEM = pl.BlockSpec(memory_space=pltpu.SMEM)
VMEM = pl.BlockSpec(memory_space=pltpu.VMEM)
BIG = pltpu.CompilerParams(vmem_limit_bytes=40 * 1024 * 1024)


def call(kernel, out_shape, inputs, name, scratch=()):
    return pl.pallas_call(
        kernel,
        out_shape=out_shape,
        in_specs=[SMEM if i.dtype == jnp.int32 else VMEM for i in inputs],
        out_specs=jax.tree.map(lambda _: VMEM, out_shape),
        scratch_shapes=scratch,
        compiler_params=BIG,
        name=name,
    )(*inputs)


def per_device(pseudo_grads, outer_params, momentum, clip_level, block_picks, cutoffs):
    z = lax.axis_index("z")
    pos = (z % 4).astype(jnp.int32).reshape(1)
    hi, lo = table_parts()
    fwd_wide = jnp.asarray(np.concatenate([hi.T, lo.T], axis=1))
    inv_wide = jnp.asarray(np.concatenate([hi, lo], axis=1))
    inv_tall = jnp.asarray(np.concatenate([hi.T, lo.T], axis=0))
    rows = pseudo_grads.shape[1]
    swap = [(NY * i + j, NX * j + i) for i in range(NX) for j in range(NY)]
    shape = jax.ShapeDtypeStruct

    picks, cuts = (
        lax.dynamic_index_in_dim(v[:, 0], lax.axis_index("x"), 1, keepdims=False) for v in (block_picks, cutoffs)
    )
    hit = picks[:, :, None] == jnp.arange(BPO, dtype=jnp.int32)
    cut = jnp.max(jnp.where(hit, cuts[:, :, None], -1), axis=1)
    cut = jnp.broadcast_to(cut.T.reshape(4, 1, BPO), (4, 4, BPO)).reshape(NZ, 1, BPO)
    cut = jnp.pad(cut, ((0, 0), (0, 0), (0, BS - BPO)))
    cut = lax.all_to_all(cut, "z", 0, 0, tiled=True)[:, 0]

    chip = pl.pallas_call(
        pack_kernel,
        out_shape=shape((NY, NC, NZ, rows, BS), BF16),
        grid=(NY,),
        in_specs=[pl.BlockSpec((None, rows, FF // NY), lambda j: (0, 0, j))],
        out_specs=pl.BlockSpec((1, NC, NZ, rows, BS), lambda j: (j, 0, 0, 0, 0)),
        compiler_params=BIG,
        name="pack",
    )(pseudo_grads)
    chip, cut = lax.optimization_barrier((chip, cut))
    cut = lax.ppermute(cut, ("x", "y"), swap)
    chip = lax.all_to_all(chip.reshape(NY * NC, NZ, rows, BS), ("x", "c"), 0, 0, tiled=True)
    spread = chip.reshape(NX, NC, NZ, rows, BS)
    spread, cut = lax.optimization_barrier((spread, cut))

    a, b = call(
        exchange_kernel,
        (shape((NX, 4, 96, BS), BF16), shape((NX, 8, 64, BS), BF16)),
        (pos, spread),
        "exchange",
    )
    pair_a, pair_b = [], []
    for g in range(0, NZ, 4):
        pair_a += [(g, g + 1), (g + 1, g), (g + 2, g + 3), (g + 3, g + 2)]
        pair_b += [(g + 1, g + 2), (g + 2, g + 1)]
    a = lax.ppermute(a, "z", pair_a)
    b = lax.ppermute(b, "z", pair_b)

    coded = call(
        forward_kernel,
        shape((NZ, BS + TAIL, BS), jnp.int16),
        (pos, cut, spread, a, b, inv_wide, fwd_wide),
        "forward",
        [pltpu.VMEM((NX, BPO, BS, BS), BF16), pltpu.VMEM((NZ, BS), F32)],
    )
    coded = lax.all_to_all(coded, "z", 0, 0, tiled=True)
    coded, norm = call(
        compact_kernel,
        (shape((BPO * BS + TAIL, BS), jnp.int16), shape((NX * NY * NC, 1, BS), F32)),
        (pos, coded),
        "compact",
    )
    coded = lax.ppermute(coded, ("x", "y"), swap)
    norm = lax.all_to_all(norm, ("x", "y", "c"), 0, 0, tiled=True)

    tile = pl.BlockSpec((3 * BS, BS), lambda i: (i, 0))
    return pl.pallas_call(
        update_kernel,
        out_shape=(shape(outer_params.shape, F32), shape(outer_params.shape, F32)),
        grid=(4,),
        in_specs=[
            tile,
            pl.BlockSpec((TAIL, BS), lambda i: (BPO * BS // TAIL, 0)),
            VMEM,
            SMEM,
            tile,
            tile,
            VMEM,
            VMEM,
        ],
        out_specs=(tile, tile),
        compiler_params=BIG,
        name="update",
    )(coded, coded, norm, clip_level, outer_params, momentum, inv_tall, inv_wide)


def solution(mesh):
    grid = Mesh(mesh.devices.reshape(NX, NY, NZ, NC), ("x", "y", "z", "c"))
    yzc = ("y", "z", "c")
    in_specs = (P("x", yzc, None), P("x", yzc), P("x", yzc), P(), P(None, yzc, None, None), P(None, yzc, None, None))
    out_specs = (P("x", yzc), P("x", yzc))
    return jax.shard_map(per_device, mesh=grid, in_specs=in_specs, out_specs=out_specs, check_vma=False)
```

```python
import functools
import math

import jax
import jax.numpy as jnp
import ml_dtypes
import numpy as np
from jax import lax
from jax.experimental import pallas as pl
from jax.experimental.pallas import tpu as pltpu
from jax.sharding import Mesh, PartitionSpec as P

BS = 128
D = 6144
FF = 16384
OUTER_RATE = 0.7
NESTEROV = 0.9
EPSILON = 1e-06
NX, NY, NZ, NC = 4, 4, 16, 2
BPO = 12
TAIL = 16
F32 = jnp.float32
BF16 = jnp.bfloat16


def table_parts():
    u = np.arange(BS, dtype=np.float64)[:, None]
    k = np.arange(BS, dtype=np.float64)[None, :]
    c = np.cos(math.pi * (2.0 * k + 1.0) * u / (2.0 * BS)) * math.sqrt(2.0 / BS)
    c[0] *= math.sqrt(0.5)
    hi = c.astype(ml_dtypes.bfloat16)
    lo = (c - hi.astype(np.float64)).astype(ml_dtypes.bfloat16)
    return hi, lo


def dot(a, b):
    return lax.dot_general(a, b, (((1,), (0,)), ((), ())), preferred_element_type=F32)


def split(v):
    hi = v.astype(BF16)
    return hi, (v - hi.astype(F32)).astype(BF16)


def times_wide(v, wide):
    hi, lo = split(v)
    both = dot(hi, wide)
    return both[:, :BS] + both[:, BS:] + dot(lo, wide[:, :BS])


def tall_times(tall, v):
    hi, lo = split(v)
    both = dot(tall, hi)
    return both[:BS] + both[BS:] + dot(tall[:BS], lo)


def pack_kernel(pos, g, *outs):
    c, x = pos[1], pos[2]
    for s in range(NX):
        for out, core in ((outs[s], c), (outs[NX + s], 1 - c)):
            base = NZ * NC * ((x + s) % 4) + core
            for m in range(4):
                for w in range(4):
                    start = pl.multiple_of((base + 2 * (4 * w + m)) * BS, BS)
                    out[4 * m + w] = g[0, :, pl.ds(start, BS)]


def by_place(pos, rows, body):
    for p in range(4):
        for c in range(2):
            mine, other = rows[:NX], rows[NX:]
            pair = (mine, other) if c == 0 else (other, mine)
            pl.when((pos[0] == p) & (pos[1] == c))(functools.partial(body, p, *pair))


def exchange_kernel(pos, *refs):
    a, b = refs[-2:]

    def body(p, los, his):
        for r in range(NX):
            lo, hi = los[r], his[r]
            if p in (0, 3):
                s = slice(0, 4) if p == 0 else slice(12, 16)
                a[r, :, 0:48] = lo[s]
                a[r, :, 48:96] = hi[s]
                continue
            for k in range(3):
                if p == 1:
                    a[r, :, 32 * k : 32 * k + 32] = lo[4 * k + 4 : 4 * k + 8, 0:32]
                else:
                    a[r, :, 32 * k : 32 * k + 32] = hi[4 * k : 4 * k + 4, 16:48]
            if p == 1:
                b[r, :, 0:16] = lo[0:8, 32:48]
                b[r, :, 16:64] = hi[0:8]
            else:
                b[r, :, 0:48] = lo[8:16]
                b[r, :, 48:64] = hi[8:16, 0:16]

    by_place(pos, refs[:-2], body)


def assemble(pos, rows, a, b, whole):
    def place(p, k, lo, hi, r):
        m = k + (k >= p)
        d = slice(4 * k, 4 * k + 4)
        s = slice(4 * m, 4 * m + 4)
        third = slice(32 * k, 32 * k + 32)
        if p == 0:
            whole[r, d, 0:48] = lo[s]
            whole[r, d, 48:96] = hi[s]
            whole[r, d, 96:128] = a[r, :, third]
        elif p == 3:
            whole[r, d, 0:32] = a[r, :, third]
            whole[r, d, 32:80] = lo[s]
            whole[r, d, 80:128] = hi[s]
        elif p == 1 and m == 0:
            whole[r, d, 0:96] = a[r]
            whole[r, d, 96:128] = lo[s, 0:32]
        elif p == 1:
            whole[r, d, 0:16] = lo[s, 32:48]
            whole[r, d, 16:64] = hi[s]
            whole[r, d, 64:128] = b[r, 4 * (m - 2) : 4 * (m - 2) + 4]
        elif m == 3:
            whole[r, d, 0:32] = hi[s, 16:48]
            whole[r, d, 32:128] = a[r]
        else:
            whole[r, d, 0:64] = b[r, s]
            whole[r, d, 64:112] = lo[s]
            whole[r, d, 112:128] = hi[s, 0:16]

    def body(p, los, his):
        for k in range(3):
            for r in range(NX):
                place(p, k, los[r], his[r], r)

    by_place(pos, rows, body)


def exponent(size):
    return jnp.clip(jnp.floor(jnp.log2(jnp.maximum(size, F32(1e-30)))) + 1.0, -100.0, 200.0)


def forward_kernel(pos, cut, *refs):
    a, b, left, wide, out, x, exps = refs[2 * NX :]
    assemble(pos, refs[: 2 * NX], a, b, x)
    p = pos[0]
    freq = lax.broadcasted_iota(jnp.int32, (BS, BS), 0) + lax.broadcasted_iota(jnp.int32, (BS, BS), 1)
    row = lax.broadcasted_iota(jnp.int32, (TAIL, BS), 0)
    exps[...] = jnp.zeros_like(exps)
    for w in range(4):
        out[4 * w + p, 0:BS] = jnp.zeros((BS, BS), jnp.int16)

    def step(w, square):
        for k in range(3):
            m = k + (k >= p).astype(jnp.int32)
            blk = p - (p > m).astype(jnp.int32)
            total = jnp.zeros((BS, BS), F32)
            for r in range(NX):
                both = dot(x[r, 4 * k + w], wide[...])
                hi, lo = split(both[:, :BS] + both[:, BS:])
                pairs = jnp.concatenate(
                    [
                        jnp.concatenate([hi, lo], axis=1),
                        jnp.concatenate([hi, jnp.zeros_like(lo)], axis=1),
                    ],
                    axis=0,
                )
                both = dot(left[...], pairs)
                coef = both[:, :BS] + both[:, BS:]
                total += jnp.where(freq <= cut[4 * w + m, 4 * blk + (pos[2] + 4 - r) % 4], coef, 0.0)
            e = exponent(jnp.max(jnp.abs(total), axis=0, keepdims=True))
            code = jnp.clip(jnp.floor(total * jnp.exp2(15.0 - e) + 0.5), -32767.0, 32767.0)
            out[4 * w + m, 0:BS] = code.astype(jnp.int32).astype(jnp.int16)
            exps[pl.ds(4 * w + m, 1), :] = e
            square += jnp.sum(total * total, axis=0, keepdims=True)
        return square

    square = jnp.zeros((1, BS), F32)
    for w in range(4):
        square = step(w, square)
    e = exponent(square)
    scaled = jnp.minimum(square, F32(3e38)) * jnp.exp2(-0.5 * e) * jnp.exp2(-0.5 * e) * 16384.0
    d1 = jnp.floor(scaled)
    d2 = jnp.floor((scaled - d1) * 16384.0)
    e = jnp.where(square > F32(3e38), 200.0, e)
    tail = jnp.where(row == 1, e, jnp.where(row == 2, d1, jnp.where(row == 3, d2, 0.0)))
    for s in range(NZ):
        mix = jnp.where(row == 0, exps[s : s + 1, :], tail)
        out[s, BS : BS + TAIL] = mix.astype(jnp.int32).astype(jnp.int16)


def compact_kernel(pos, z, out, norm):
    p = pos[0]
    row = lax.broadcasted_iota(jnp.int32, (TAIL, BS), 0)
    tail = jnp.zeros((TAIL, BS), F32)
    for g in range(4):
        for blk in range(3):
            src = 4 * g + blk + (p <= blk).astype(jnp.int32)
            n = 3 * g + blk
            out[BS * n : BS * n + BS] = z[src, 0:BS]
            e = z[src, BS : BS + TAIL].astype(jnp.int32).astype(F32)[0:1]
            tail = jnp.where(row == n, e, tail)
    out[BS * BPO : BS * BPO + TAIL] = tail.astype(jnp.int32).astype(jnp.int16)
    total = jnp.zeros((1, BS), F32)
    for s in range(NZ):
        t = z[s, BS : BS + TAIL].astype(jnp.int32).astype(F32)
        part = t[2:3] * F32(1.0 / 16384.0) + t[3:4] * F32(1.0 / 16384.0**2)
        total += part * jnp.exp2(0.5 * t[1:2]) * jnp.exp2(0.5 * t[1:2])
    norm[...] = jnp.broadcast_to(total[None], norm.shape)


def update_kernel(code, tail, norm, clip, params, mom, tall, wide, new_p, new_m):
    i = pl.program_id(0)
    total = jnp.sum(jnp.sum(norm[...], axis=0), axis=1, keepdims=True)
    factor = jnp.minimum(F32(1.0), clip[0] * F32(math.sqrt(D * FF)) / (jnp.sqrt(total) + F32(EPSILON)))
    row = lax.broadcasted_iota(jnp.int32, (TAIL, BS), 0)
    exps = tail[...].astype(jnp.int32).astype(F32)
    for n in range(3):
        e = jnp.sum(jnp.where(row == 3 * i + n, exps, 0.0), axis=0, keepdims=True)
        d = slice(BS * n, BS * n + BS)
        coef = code[d].astype(jnp.int32).astype(F32) * (jnp.exp2(e - 15.0) * factor)
        upd = tall_times(tall[...], times_wide(coef, wide[...]))
        nm = NESTEROV * mom[d] + upd
        new_m[d] = nm
        new_p[d] = params[d] - OUTER_RATE * (upd + NESTEROV * nm)


SMEM = pl.BlockSpec(memory_space=pltpu.SMEM)
VMEM = pl.BlockSpec(memory_space=pltpu.VMEM)
BIG = pltpu.CompilerParams(vmem_limit_bytes=40 * 1024 * 1024)


def call(kernel, out_shape, inputs, name, scratch=()):
    return pl.pallas_call(
        kernel,
        out_shape=out_shape,
        in_specs=[SMEM if i.dtype == jnp.int32 else VMEM for i in inputs],
        out_specs=jax.tree.map(lambda _: VMEM, out_shape),
        scratch_shapes=scratch,
        compiler_params=BIG,
        name=name,
    )(*inputs)


def per_device(pseudo_grads, outer_params, momentum, clip_level, block_picks, cutoffs):
    z = lax.axis_index("z")
    pos = jnp.stack([z % 4, lax.axis_index("c"), lax.axis_index("x")]).astype(jnp.int32)
    hi, lo = table_parts()
    fwd_wide = jnp.asarray(np.concatenate([hi.T, lo.T], axis=1))
    inv_wide = jnp.asarray(np.concatenate([hi, lo], axis=1))
    inv_tall = jnp.asarray(np.concatenate([hi.T, lo.T], axis=0))
    rows = pseudo_grads.shape[1]
    swap = [(NY * i + j, NX * j + i) for i in range(NX) for j in range(NY)]
    shape = jax.ShapeDtypeStruct

    picks, cuts = (
        lax.dynamic_index_in_dim(v[:, 0], lax.axis_index("x"), 1, keepdims=False) for v in (block_picks, cutoffs)
    )
    hit = picks[:, :, None] == jnp.arange(BPO, dtype=jnp.int32)
    cut = jnp.max(jnp.where(hit, cuts[:, :, None], -1), axis=1)
    cut = jnp.broadcast_to(cut.T.reshape(4, 1, BPO), (4, 4, BPO)).reshape(NZ, 1, BPO)
    cut = jnp.pad(cut, ((0, 0), (0, 0), (0, BS - BPO)))
    cut, pseudo_grads = lax.optimization_barrier((cut, pseudo_grads))
    cut = lax.all_to_all(cut, "z", 0, 0, tiled=True)[:, 0]

    packed = call(
        pack_kernel, [shape((NZ, rows, BS), BF16)] * (2 * NX), (pos, pseudo_grads), "pack"
    )
    spread = list(packed)
    for n in (NX + 2, 2, NX + 1, NX + 3, 1, 3, NX):
        flip, step = divmod(n, NX)
        pairs = [
            (NC * i + c, NC * ((i + step) % NX) + (c ^ flip)) for i in range(NX) for c in range(NC)
        ]
        spread[n] = lax.ppermute(packed[n], ("x", "c"), pairs)
    *spread, cut = lax.optimization_barrier((*spread, cut))
    cut = lax.ppermute(cut, ("x", "y"), swap)

    a, b = call(
        exchange_kernel,
        (shape((NX, 4, 96, BS), BF16), shape((NX, 8, 64, BS), BF16)),
        (pos, *spread),
        "exchange",
    )
    pair_a, pair_b = [], []
    for g in range(0, NZ, 4):
        pair_a += [(g, g + 1), (g + 1, g), (g + 2, g + 3), (g + 3, g + 2)]
        pair_b += [(g + 1, g + 2), (g + 2, g + 1)]
    a = lax.ppermute(a, "z", pair_a)
    b = lax.ppermute(b, "z", pair_b)

    coded = call(
        forward_kernel,
        shape((NZ, BS + TAIL, BS), jnp.int16),
        (pos, cut, *spread, a, b, inv_wide, fwd_wide),
        "forward",
        [pltpu.VMEM((NX, BPO, BS, BS), BF16), pltpu.VMEM((NZ, BS), F32)],
    )
    coded = lax.all_to_all(coded, "z", 0, 0, tiled=True)
    coded, norm = call(
        compact_kernel,
        (shape((BPO * BS + TAIL, BS), jnp.int16), shape((NX * NY * NC, 1, BS), F32)),
        (pos, coded),
        "compact",
    )
    coded = lax.ppermute(coded, ("x", "y"), swap)
    norm = lax.all_to_all(norm, ("x", "y", "c"), 0, 0, tiled=True)

    tile = pl.BlockSpec((3 * BS, BS), lambda i: (i, 0))
    return pl.pallas_call(
        update_kernel,
        out_shape=(shape(outer_params.shape, F32), shape(outer_params.shape, F32)),
        grid=(4,),
        in_specs=[
            tile,
            pl.BlockSpec((TAIL, BS), lambda i: (BPO * BS // TAIL, 0)),
            VMEM,
            SMEM,
            tile,
            tile,
            VMEM,
            VMEM,
        ],
        out_specs=(tile, tile),
        compiler_params=BIG,
        name="update",
    )(coded, coded, norm, clip_level, outer_params, momentum, inv_tall, inv_wide)


def solution(mesh):
    grid = Mesh(mesh.devices.reshape(NX, NY, NZ, NC), ("x", "y", "z", "c"))
    yzc = ("y", "z", "c")
    in_specs = (P("x", yzc, None), P("x", yzc), P("x", yzc), P(), P(None, yzc, None, None), P(None, yzc, None, None))
    out_specs = (P("x", yzc), P("x", yzc))
    return jax.shard_map(per_device, mesh=grid, in_specs=in_specs, out_specs=out_specs, check_vma=False)
```

```python
import functools
import math

import jax
import jax.numpy as jnp
import ml_dtypes
import numpy as np
from jax import lax
from jax.experimental import pallas as pl
from jax.experimental.pallas import tpu as pltpu
from jax.sharding import Mesh, PartitionSpec as P

BS = 128
D = 6144
FF = 16384
OUTER_RATE = 0.7
NESTEROV = 0.9
EPSILON = 1e-06
NX, NY, NZ, NC = 4, 4, 16, 2
BPO = 12
TAIL = 16
F32 = jnp.float32
BF16 = jnp.bfloat16


def table_parts():
    u = np.arange(BS, dtype=np.float64)[:, None]
    k = np.arange(BS, dtype=np.float64)[None, :]
    c = np.cos(math.pi * (2.0 * k + 1.0) * u / (2.0 * BS)) * math.sqrt(2.0 / BS)
    c[0] *= math.sqrt(0.5)
    hi = c.astype(ml_dtypes.bfloat16)
    lo = (c - hi.astype(np.float64)).astype(ml_dtypes.bfloat16)
    return hi, lo


def dot(a, b):
    return lax.dot_general(a, b, (((1,), (0,)), ((), ())), preferred_element_type=F32)


def split(v):
    hi = v.astype(BF16)
    return hi, (v - hi.astype(F32)).astype(BF16)


def times_wide(v, wide):
    hi, lo = split(v)
    both = dot(hi, wide)
    return both[:, :BS] + both[:, BS:] + dot(lo, wide[:, :BS])


def tall_times(tall, v):
    hi, lo = split(v)
    both = dot(tall, hi)
    return both[:BS] + both[BS:] + dot(tall[:BS], lo)


def pack_kernel(pos, g, *outs):
    c, x = pos[1], pos[2]
    for s in range(NX):
        for half, core in enumerate((c, 1 - c)):
            base = NZ * NC * ((x + s) % 4) + core
            for m in range(4):
                for w in range(4):
                    start = pl.multiple_of((base + 2 * (4 * w + m)) * BS, BS)
                    outs[s][half, 4 * m + w] = g[0, :, pl.ds(start, BS)]


def give_kernel(*refs):
    for s in range(NX):
        refs[NX][s] = refs[s][1]


def by_place(pos, rows, body):
    for p in range(4):
        for c in range(2):
            mine = [v.at[0] for v in rows[:NX]]
            other = [rows[NX].at[s] for s in range(NX)]
            pair = (mine, other) if c == 0 else (other, mine)
            pl.when((pos[0] == p) & (pos[1] == c))(functools.partial(body, p, *pair))


def exchange_kernel(pos, *refs):
    a, b = refs[-2:]

    def body(p, los, his):
        for r in range(NX):
            lo, hi = los[r], his[r]
            if p in (0, 3):
                s = slice(0, 4) if p == 0 else slice(12, 16)
                a[r, :, 0:48] = lo[s]
                a[r, :, 48:96] = hi[s]
                continue
            for k in range(3):
                if p == 1:
                    a[r, :, 32 * k : 32 * k + 32] = lo[4 * k + 4 : 4 * k + 8, 0:32]
                else:
                    a[r, :, 32 * k : 32 * k + 32] = hi[4 * k : 4 * k + 4, 16:48]
            if p == 1:
                b[r, :, 0:16] = lo[0:8, 32:48]
                b[r, :, 16:64] = hi[0:8]
            else:
                b[r, :, 0:48] = lo[8:16]
                b[r, :, 48:64] = hi[8:16, 0:16]

    by_place(pos, refs[:-2], body)


def assemble(pos, rows, a, b, whole):
    def place(p, k, lo, hi, r):
        m = k + (k >= p)
        d = slice(4 * k, 4 * k + 4)
        s = slice(4 * m, 4 * m + 4)
        third = slice(32 * k, 32 * k + 32)
        if p == 0:
            whole[r, d, 0:48] = lo[s]
            whole[r, d, 48:96] = hi[s]
            whole[r, d, 96:128] = a[r, :, third]
        elif p == 3:
            whole[r, d, 0:32] = a[r, :, third]
            whole[r, d, 32:80] = lo[s]
            whole[r, d, 80:128] = hi[s]
        elif p == 1 and m == 0:
            whole[r, d, 0:96] = a[r]
            whole[r, d, 96:128] = lo[s, 0:32]
        elif p == 1:
            whole[r, d, 0:16] = lo[s, 32:48]
            whole[r, d, 16:64] = hi[s]
            whole[r, d, 64:128] = b[r, 4 * (m - 2) : 4 * (m - 2) + 4]
        elif m == 3:
            whole[r, d, 0:32] = hi[s, 16:48]
            whole[r, d, 32:128] = a[r]
        else:
            whole[r, d, 0:64] = b[r, s]
            whole[r, d, 64:112] = lo[s]
            whole[r, d, 112:128] = hi[s, 0:16]

    def body(p, los, his):
        for k in range(3):
            for r in range(NX):
                place(p, k, los[r], his[r], r)

    by_place(pos, rows, body)


def exponent(size):
    return jnp.clip(jnp.floor(jnp.log2(jnp.maximum(size, F32(1e-30)))) + 1.0, -100.0, 200.0)


def forward_kernel(pos, cut, *refs):
    a, b, left, wide, out, x, exps = refs[NX + 1 :]
    assemble(pos, refs[: NX + 1], a, b, x)
    p = pos[0]
    freq = lax.broadcasted_iota(jnp.int32, (BS, BS), 0) + lax.broadcasted_iota(jnp.int32, (BS, BS), 1)
    row = lax.broadcasted_iota(jnp.int32, (TAIL, BS), 0)
    exps[...] = jnp.zeros_like(exps)
    for w in range(4):
        out[4 * w + p, 0:BS] = jnp.zeros((BS, BS), jnp.int16)

    def step(w, square):
        for k in range(3):
            m = k + (k >= p).astype(jnp.int32)
            blk = p - (p > m).astype(jnp.int32)
            total = jnp.zeros((BS, BS), F32)
            for r in range(NX):
                both = dot(x[r, 4 * k + w], wide[...])
                hi, lo = split(both[:, :BS] + both[:, BS:])
                pairs = jnp.concatenate(
                    [
                        jnp.concatenate([hi, lo], axis=1),
                        jnp.concatenate([hi, jnp.zeros_like(lo)], axis=1),
                    ],
                    axis=0,
                )
                both = dot(left[...], pairs)
                coef = both[:, :BS] + both[:, BS:]
                total += jnp.where(freq <= cut[4 * w + m, 4 * blk + (pos[2] + 4 - r) % 4], coef, 0.0)
            e = exponent(jnp.max(jnp.abs(total), axis=0, keepdims=True))
            code = jnp.clip(jnp.floor(total * jnp.exp2(15.0 - e) + 0.5), -32767.0, 32767.0)
            out[4 * w + m, 0:BS] = code.astype(jnp.int32).astype(jnp.int16)
            exps[pl.ds(4 * w + m, 1), :] = e
            square += jnp.sum(total * total, axis=0, keepdims=True)
        return square

    square = jnp.zeros((1, BS), F32)
    for w in range(4):
        square = step(w, square)
    e = exponent(square)
    scaled = jnp.minimum(square, F32(3e38)) * jnp.exp2(-0.5 * e) * jnp.exp2(-0.5 * e) * 16384.0
    d1 = jnp.floor(scaled)
    d2 = jnp.floor((scaled - d1) * 16384.0)
    e = jnp.where(square > F32(3e38), 200.0, e)
    tail = jnp.where(row == 1, e, jnp.where(row == 2, d1, jnp.where(row == 3, d2, 0.0)))
    for s in range(NZ):
        mix = jnp.where(row == 0, exps[s : s + 1, :], tail)
        out[s, BS : BS + TAIL] = mix.astype(jnp.int32).astype(jnp.int16)


def compact_kernel(pos, z, out, norm):
    p = pos[0]
    row = lax.broadcasted_iota(jnp.int32, (TAIL, BS), 0)
    tail = jnp.zeros((TAIL, BS), F32)
    for g in range(4):
        for blk in range(3):
            src = 4 * g + blk + (p <= blk).astype(jnp.int32)
            n = 3 * g + blk
            out[BS * n : BS * n + BS] = z[src, 0:BS]
            e = z[src, BS : BS + TAIL].astype(jnp.int32).astype(F32)[0:1]
            tail = jnp.where(row == n, e, tail)
    out[BS * BPO : BS * BPO + TAIL] = tail.astype(jnp.int32).astype(jnp.int16)
    total = jnp.zeros((1, BS), F32)
    for s in range(NZ):
        t = z[s, BS : BS + TAIL].astype(jnp.int32).astype(F32)
        part = t[2:3] * F32(1.0 / 16384.0) + t[3:4] * F32(1.0 / 16384.0**2)
        total += part * jnp.exp2(0.5 * t[1:2]) * jnp.exp2(0.5 * t[1:2])
    norm[...] = jnp.broadcast_to(total[None], norm.shape)


def update_kernel(code, tail, norm, clip, params, mom, tall, wide, new_p, new_m):
    i = pl.program_id(0)
    total = jnp.sum(jnp.sum(norm[...], axis=0), axis=1, keepdims=True)
    factor = jnp.minimum(F32(1.0), clip[0] * F32(math.sqrt(D * FF)) / (jnp.sqrt(total) + F32(EPSILON)))
    row = lax.broadcasted_iota(jnp.int32, (TAIL, BS), 0)
    exps = tail[...].astype(jnp.int32).astype(F32)
    for n in range(3):
        e = jnp.sum(jnp.where(row == 3 * i + n, exps, 0.0), axis=0, keepdims=True)
        d = slice(BS * n, BS * n + BS)
        coef = code[d].astype(jnp.int32).astype(F32) * (jnp.exp2(e - 15.0) * factor)
        upd = tall_times(tall[...], times_wide(coef, wide[...]))
        nm = NESTEROV * mom[d] + upd
        new_m[d] = nm
        new_p[d] = params[d] - OUTER_RATE * (upd + NESTEROV * nm)


SMEM = pl.BlockSpec(memory_space=pltpu.SMEM)
VMEM = pl.BlockSpec(memory_space=pltpu.VMEM)
BIG = pltpu.CompilerParams(vmem_limit_bytes=40 * 1024 * 1024)


def call(kernel, out_shape, inputs, name, scratch=()):
    return pl.pallas_call(
        kernel,
        out_shape=out_shape,
        in_specs=[SMEM if i.dtype == jnp.int32 else VMEM for i in inputs],
        out_specs=jax.tree.map(lambda _: VMEM, out_shape),
        scratch_shapes=scratch,
        compiler_params=BIG,
        name=name,
    )(*inputs)


def per_device(pseudo_grads, outer_params, momentum, clip_level, block_picks, cutoffs):
    z = lax.axis_index("z")
    pos = jnp.stack([z % 4, lax.axis_index("c"), lax.axis_index("x")]).astype(jnp.int32)
    hi, lo = table_parts()
    fwd_wide = jnp.asarray(np.concatenate([hi.T, lo.T], axis=1))
    inv_wide = jnp.asarray(np.concatenate([hi, lo], axis=1))
    inv_tall = jnp.asarray(np.concatenate([hi.T, lo.T], axis=0))
    rows = pseudo_grads.shape[1]
    swap = [(NY * i + j, NX * j + i) for i in range(NX) for j in range(NY)]
    shape = jax.ShapeDtypeStruct

    picks, cuts = (
        lax.dynamic_index_in_dim(v[:, 0], lax.axis_index("x"), 1, keepdims=False) for v in (block_picks, cutoffs)
    )
    hit = picks[:, :, None] == jnp.arange(BPO, dtype=jnp.int32)
    cut = jnp.max(jnp.where(hit, cuts[:, :, None], -1), axis=1)
    cut = jnp.broadcast_to(cut.T.reshape(4, 1, BPO), (4, 4, BPO)).reshape(NZ, 1, BPO)
    cut = jnp.pad(cut, ((0, 0), (0, 0), (0, BS - BPO)))
    cut, pseudo_grads = lax.optimization_barrier((cut, pseudo_grads))
    cut = lax.all_to_all(cut, "z", 0, 0, tiled=True)[:, 0]

    packed = call(pack_kernel, [shape((NC, NZ, rows, BS), BF16)] * NX, (pos, pseudo_grads), "pack")
    spread = [packed[0]] + [
        lax.ppermute(packed[n], "x", [(i, (i + n) % NX) for i in range(NX)]) for n in range(1, NX)
    ]
    *spread, cut = lax.optimization_barrier((*spread, cut))
    give = call(give_kernel, shape((NX, NZ, rows, BS), BF16), spread, "give")
    spread.append(lax.ppermute(give, "c", [(0, 1), (1, 0)]))
    cut = lax.ppermute(cut, ("x", "y"), swap)

    a, b = call(
        exchange_kernel,
        (shape((NX, 4, 96, BS), BF16), shape((NX, 8, 64, BS), BF16)),
        (pos, *spread),
        "exchange",
    )
    pair_a, pair_b = [], []
    for g in range(0, NZ, 4):
        pair_a += [(g, g + 1), (g + 1, g), (g + 2, g + 3), (g + 3, g + 2)]
        pair_b += [(g + 1, g + 2), (g + 2, g + 1)]
    a = lax.ppermute(a, "z", pair_a)
    b = lax.ppermute(b, "z", pair_b)

    coded = call(
        forward_kernel,
        shape((NZ, BS + TAIL, BS), jnp.int16),
        (pos, cut, *spread, a, b, inv_wide, fwd_wide),
        "forward",
        [pltpu.VMEM((NX, BPO, BS, BS), BF16), pltpu.VMEM((NZ, BS), F32)],
    )
    coded = lax.all_to_all(coded, "z", 0, 0, tiled=True)
    coded, norm = call(
        compact_kernel,
        (shape((BPO * BS + TAIL, BS), jnp.int16), shape((NX * NY * NC, 1, BS), F32)),
        (pos, coded),
        "compact",
    )
    coded = lax.ppermute(coded, ("x", "y"), swap)
    norm = lax.all_to_all(norm, ("x", "y", "c"), 0, 0, tiled=True)

    tile = pl.BlockSpec((3 * BS, BS), lambda i: (i, 0))
    return pl.pallas_call(
        update_kernel,
        out_shape=(shape(outer_params.shape, F32), shape(outer_params.shape, F32)),
        grid=(4,),
        in_specs=[
            tile,
            pl.BlockSpec((TAIL, BS), lambda i: (BPO * BS // TAIL, 0)),
            VMEM,
            SMEM,
            tile,
            tile,
            VMEM,
            VMEM,
        ],
        out_specs=(tile, tile),
        compiler_params=BIG,
        name="update",
    )(coded, coded, norm, clip_level, outer_params, momentum, inv_tall, inv_wide)


def solution(mesh):
    grid = Mesh(mesh.devices.reshape(NX, NY, NZ, NC), ("x", "y", "z", "c"))
    yzc = ("y", "z", "c")
    in_specs = (P("x", yzc, None), P("x", yzc), P("x", yzc), P(), P(None, yzc, None, None), P(None, yzc, None, None))
    out_specs = (P("x", yzc), P("x", yzc))
    return jax.shard_map(per_device, mesh=grid, in_specs=in_specs, out_specs=out_specs, check_vma=False)
```

```python
import functools
import math

import jax
import jax.numpy as jnp
import ml_dtypes
import numpy as np
from jax import lax
from jax.experimental import pallas as pl
from jax.experimental.pallas import tpu as pltpu
from jax.sharding import Mesh, PartitionSpec as P

BS = 128
D = 6144
FF = 16384
OUTER_RATE = 0.7
NESTEROV = 0.9
EPSILON = 1e-06
NX, NY, NZ, NC = 4, 4, 16, 2
BPO = 12
TAIL = 16
F32 = jnp.float32
BF16 = jnp.bfloat16


def table_parts():
    u = np.arange(BS, dtype=np.float64)[:, None]
    k = np.arange(BS, dtype=np.float64)[None, :]
    c = np.cos(math.pi * (2.0 * k + 1.0) * u / (2.0 * BS)) * math.sqrt(2.0 / BS)
    c[0] *= math.sqrt(0.5)
    hi = c.astype(ml_dtypes.bfloat16)
    lo = (c - hi.astype(np.float64)).astype(ml_dtypes.bfloat16)
    return hi, lo


def dot(a, b):
    return lax.dot_general(a, b, (((1,), (0,)), ((), ())), preferred_element_type=F32)


def split(v):
    hi = v.astype(BF16)
    return hi, (v - hi.astype(F32)).astype(BF16)


def times_wide(v, wide):
    hi, lo = split(v)
    both = dot(hi, wide)
    return both[:, :BS] + both[:, BS:] + dot(lo, wide[:, :BS])


def tall_times(tall, v):
    hi, lo = split(v)
    both = dot(tall, hi)
    return both[:BS] + both[BS:] + dot(tall[:BS], lo)


def pack_kernel(pos, g, *outs):
    c, x = pos[1], pos[2]
    for s in range(NX):
        for half, core in enumerate((c, 1 - c)):
            base = NZ * NC * ((x + s) % 4) + core
            for m in range(4):
                for w in range(4):
                    start = pl.multiple_of((base + 2 * (4 * w + m)) * BS, BS)
                    outs[s][half, 4 * m + w] = g[0, :, pl.ds(start, BS)]


def give_kernel(*refs):
    for s in range(NX):
        refs[NX][s] = refs[s][1]


def by_place(pos, rows, body):
    for p in range(4):
        for c in range(2):
            mine = [v.at[0] for v in rows[:NX]]
            other = [rows[NX].at[s] for s in range(NX)]
            pair = (mine, other) if c == 0 else (other, mine)
            pl.when((pos[0] == p) & (pos[1] == c))(functools.partial(body, p, *pair))


def exchange_kernel(pos, *refs):
    a, b = refs[-2:]

    def body(p, los, his):
        for r in range(NX):
            lo, hi = los[r], his[r]
            if p in (0, 3):
                s = slice(0, 4) if p == 0 else slice(12, 16)
                a[r, :, 0:48] = lo[s]
                a[r, :, 48:96] = hi[s]
                continue
            for k in range(3):
                if p == 1:
                    a[r, :, 32 * k : 32 * k + 32] = lo[4 * k + 4 : 4 * k + 8, 0:32]
                else:
                    a[r, :, 32 * k : 32 * k + 32] = hi[4 * k : 4 * k + 4, 16:48]
            if p == 1:
                b[r, :, 0:16] = lo[0:8, 32:48]
                b[r, :, 16:64] = hi[0:8]
            else:
                b[r, :, 0:48] = lo[8:16]
                b[r, :, 48:64] = hi[8:16, 0:16]

    by_place(pos, refs[:-2], body)


def assemble(pos, rows, a, b, whole):
    def place(p, k, lo, hi, r):
        m = k + (k >= p)
        d = slice(4 * k, 4 * k + 4)
        s = slice(4 * m, 4 * m + 4)
        third = slice(32 * k, 32 * k + 32)
        if p == 0:
            whole[r, d, 0:48] = lo[s]
            whole[r, d, 48:96] = hi[s]
            whole[r, d, 96:128] = a[r, :, third]
        elif p == 3:
            whole[r, d, 0:32] = a[r, :, third]
            whole[r, d, 32:80] = lo[s]
            whole[r, d, 80:128] = hi[s]
        elif p == 1 and m == 0:
            whole[r, d, 0:96] = a[r]
            whole[r, d, 96:128] = lo[s, 0:32]
        elif p == 1:
            whole[r, d, 0:16] = lo[s, 32:48]
            whole[r, d, 16:64] = hi[s]
            whole[r, d, 64:128] = b[r, 4 * (m - 2) : 4 * (m - 2) + 4]
        elif m == 3:
            whole[r, d, 0:32] = hi[s, 16:48]
            whole[r, d, 32:128] = a[r]
        else:
            whole[r, d, 0:64] = b[r, s]
            whole[r, d, 64:112] = lo[s]
            whole[r, d, 112:128] = hi[s, 0:16]

    def body(p, los, his):
        for k in range(3):
            for r in range(NX):
                place(p, k, los[r], his[r], r)

    by_place(pos, rows, body)


def exponent(size):
    return jnp.clip(jnp.floor(jnp.log2(jnp.maximum(size, F32(1e-30)))) + 1.0, -100.0, 200.0)


def forward_kernel(pos, cut, *refs):
    a, b, left, wide, out, norm, x, exps = refs[NX + 1 :]
    assemble(pos, refs[: NX + 1], a, b, x)
    p = pos[0]
    freq = lax.broadcasted_iota(jnp.int32, (BS, BS), 0) + lax.broadcasted_iota(jnp.int32, (BS, BS), 1)
    row = lax.broadcasted_iota(jnp.int32, (TAIL, BS), 0)
    exps[...] = jnp.zeros_like(exps)
    for w in range(4):
        out[4 * w + p, 0:BS] = jnp.zeros((BS, BS), jnp.int16)

    def step(w, square):
        for k in range(3):
            m = k + (k >= p).astype(jnp.int32)
            blk = p - (p > m).astype(jnp.int32)
            total = jnp.zeros((BS, BS), F32)
            for r in range(NX):
                both = dot(x[r, 4 * k + w], wide[...])
                hi, lo = split(both[:, :BS] + both[:, BS:])
                pairs = jnp.concatenate(
                    [
                        jnp.concatenate([hi, lo], axis=1),
                        jnp.concatenate([hi, jnp.zeros_like(lo)], axis=1),
                    ],
                    axis=0,
                )
                both = dot(left[...], pairs)
                coef = both[:, :BS] + both[:, BS:]
                total += jnp.where(freq <= cut[4 * w + m, 4 * blk + (pos[2] + 4 - r) % 4], coef, 0.0)
            e = exponent(jnp.max(jnp.abs(total), axis=0, keepdims=True))
            code = jnp.clip(jnp.floor(total * jnp.exp2(15.0 - e) + 0.5), -32767.0, 32767.0)
            out[4 * w + m, 0:BS] = code.astype(jnp.int32).astype(jnp.int16)
            exps[pl.ds(4 * w + m, 1), :] = e
            square += jnp.sum(total * total, axis=0, keepdims=True)
        return square

    square = jnp.zeros((1, BS), F32)
    for w in range(4):
        square = step(w, square)
    norm[...] = square
    for s in range(NZ):
        tail = jnp.where(row == 0, exps[s : s + 1, :], 0.0)
        out[s, BS : BS + TAIL] = tail.astype(jnp.int32).astype(jnp.int16)


def compact_kernel(pos, z, out):
    p = pos[0]
    row = lax.broadcasted_iota(jnp.int32, (TAIL, BS), 0)
    tail = jnp.zeros((TAIL, BS), F32)
    for g in range(4):
        for blk in range(3):
            src = 4 * g + blk + (p <= blk).astype(jnp.int32)
            n = 3 * g + blk
            out[BS * n : BS * n + BS] = z[src, 0:BS]
            e = z[src, BS : BS + TAIL].astype(jnp.int32).astype(F32)[0:1]
            tail = jnp.where(row == n, e, tail)
    out[BS * BPO : BS * BPO + TAIL] = tail.astype(jnp.int32).astype(jnp.int16)


def update_kernel(code, tail, norm, clip, params, mom, tall, wide, new_p, new_m):
    i = pl.program_id(0)
    total = jnp.sum(jnp.sum(norm[...], axis=0), axis=1, keepdims=True)
    factor = jnp.minimum(F32(1.0), clip[0] * F32(math.sqrt(D * FF)) / (jnp.sqrt(total) + F32(EPSILON)))
    row = lax.broadcasted_iota(jnp.int32, (TAIL, BS), 0)
    exps = tail[...].astype(jnp.int32).astype(F32)
    for n in range(3):
        e = jnp.sum(jnp.where(row == 3 * i + n, exps, 0.0), axis=0, keepdims=True)
        d = slice(BS * n, BS * n + BS)
        coef = code[d].astype(jnp.int32).astype(F32) * (jnp.exp2(e - 15.0) * factor)
        upd = tall_times(tall[...], times_wide(coef, wide[...]))
        nm = NESTEROV * mom[d] + upd
        new_m[d] = nm
        new_p[d] = params[d] - OUTER_RATE * (upd + NESTEROV * nm)


SMEM = pl.BlockSpec(memory_space=pltpu.SMEM)
VMEM = pl.BlockSpec(memory_space=pltpu.VMEM)
BIG = pltpu.CompilerParams(vmem_limit_bytes=40 * 1024 * 1024)


def call(kernel, out_shape, inputs, name, scratch=()):
    return pl.pallas_call(
        kernel,
        out_shape=out_shape,
        in_specs=[SMEM if i.dtype == jnp.int32 else VMEM for i in inputs],
        out_specs=jax.tree.map(lambda _: VMEM, out_shape),
        scratch_shapes=scratch,
        compiler_params=BIG,
        name=name,
    )(*inputs)


def per_device(pseudo_grads, outer_params, momentum, clip_level, block_picks, cutoffs):
    z = lax.axis_index("z")
    pos = jnp.stack([z % 4, lax.axis_index("c"), lax.axis_index("x")]).astype(jnp.int32)
    hi, lo = table_parts()
    fwd_wide = jnp.asarray(np.concatenate([hi.T, lo.T], axis=1))
    inv_wide = jnp.asarray(np.concatenate([hi, lo], axis=1))
    inv_tall = jnp.asarray(np.concatenate([hi.T, lo.T], axis=0))
    rows = pseudo_grads.shape[1]
    swap = [(NY * i + j, NX * j + i) for i in range(NX) for j in range(NY)]
    shape = jax.ShapeDtypeStruct

    picks, cuts = (
        lax.dynamic_index_in_dim(v[:, 0], lax.axis_index("x"), 1, keepdims=False) for v in (block_picks, cutoffs)
    )
    hit = picks[:, :, None] == jnp.arange(BPO, dtype=jnp.int32)
    cut = jnp.max(jnp.where(hit, cuts[:, :, None], -1), axis=1)
    cut = jnp.broadcast_to(cut.T.reshape(4, 1, BPO), (4, 4, BPO)).reshape(NZ, 1, BPO)
    cut = jnp.pad(cut, ((0, 0), (0, 0), (0, BS - BPO)))

    packed = call(pack_kernel, [shape((NC, NZ, rows, BS), BF16)] * NX, (pos, pseudo_grads), "pack")
    *packed, cut = lax.optimization_barrier((*packed, cut))
    cut = lax.all_to_all(cut, "z", 0, 0, tiled=True)[:, 0]
    spread = [packed[0]] + [
        lax.ppermute(packed[n], "x", [(i, (i + n) % NX) for i in range(NX)]) for n in range(1, NX)
    ]
    *spread, cut = lax.optimization_barrier((*spread, cut))
    give = call(give_kernel, shape((NX, NZ, rows, BS), BF16), spread, "give")
    spread.append(lax.ppermute(give, "c", [(0, 1), (1, 0)]))
    cut = lax.ppermute(cut, ("x", "y"), swap)

    a, b = call(
        exchange_kernel,
        (shape((NX, 4, 96, BS), BF16), shape((NX, 8, 64, BS), BF16)),
        (pos, *spread),
        "exchange",
    )
    pair_a, pair_b = [], []
    for g in range(0, NZ, 4):
        pair_a += [(g, g + 1), (g + 1, g), (g + 2, g + 3), (g + 3, g + 2)]
        pair_b += [(g + 1, g + 2), (g + 2, g + 1)]
    a = lax.ppermute(a, "z", pair_a)
    b = lax.ppermute(b, "z", pair_b)

    coded, square = call(
        forward_kernel,
        (shape((NZ, BS + TAIL, BS), jnp.int16), shape((1, BS), F32)),
        (pos, cut, *spread, a, b, inv_wide, fwd_wide),
        "forward",
        [pltpu.VMEM((NX, BPO, BS, BS), BF16), pltpu.VMEM((NZ, BS), F32)],
    )
    coded = lax.all_to_all(coded, "z", 0, 0, tiled=True)
    for axis, size, bit in (("c", NC, 1), ("x", NX, 1), ("y", NY, 1), ("x", NX, 2), ("y", NY, 2)):
        square += lax.ppermute(square, axis, [(i, i ^ bit) for i in range(size)])
    coded, square = lax.optimization_barrier((coded, square))
    coded = call(compact_kernel, shape((BPO * BS + TAIL, BS), jnp.int16), (pos, coded), "compact")
    coded = lax.ppermute(coded, ("x", "y"), swap)
    norm = lax.all_to_all(jnp.broadcast_to(square[None], (NZ, 1, BS)), "z", 0, 0, tiled=True)

    tile = pl.BlockSpec((3 * BS, BS), lambda i: (i, 0))
    return pl.pallas_call(
        update_kernel,
        out_shape=(shape(outer_params.shape, F32), shape(outer_params.shape, F32)),
        grid=(4,),
        in_specs=[
            tile,
            pl.BlockSpec((TAIL, BS), lambda i: (BPO * BS // TAIL, 0)),
            VMEM,
            SMEM,
            tile,
            tile,
            VMEM,
            VMEM,
        ],
        out_specs=(tile, tile),
        compiler_params=BIG,
        name="update",
    )(coded, coded, norm, clip_level, outer_params, momentum, inv_tall, inv_wide)


def solution(mesh):
    grid = Mesh(mesh.devices.reshape(NX, NY, NZ, NC), ("x", "y", "z", "c"))
    yzc = ("y", "z", "c")
    in_specs = (P("x", yzc, None), P("x", yzc), P("x", yzc), P(), P(None, yzc, None, None), P(None, yzc, None, None))
    out_specs = (P("x", yzc), P("x", yzc))
    return jax.shard_map(per_device, mesh=grid, in_specs=in_specs, out_specs=out_specs, check_vma=False)
```

```python
import functools
import math

import jax
import jax.numpy as jnp
import ml_dtypes
import numpy as np
from jax import lax
from jax.experimental import pallas as pl
from jax.experimental.pallas import tpu as pltpu
from jax.sharding import Mesh, PartitionSpec as P

BS = 128
D = 6144
FF = 16384
OUTER_RATE = 0.7
NESTEROV = 0.9
EPSILON = 1e-06
NX, NY, NZ, NC = 4, 4, 16, 2
BPO = 12
TAIL = 16
F32 = jnp.float32
BF16 = jnp.bfloat16


def table_parts():
    u = np.arange(BS, dtype=np.float64)[:, None]
    k = np.arange(BS, dtype=np.float64)[None, :]
    c = np.cos(math.pi * (2.0 * k + 1.0) * u / (2.0 * BS)) * math.sqrt(2.0 / BS)
    c[0] *= math.sqrt(0.5)
    hi = c.astype(ml_dtypes.bfloat16)
    lo = (c - hi.astype(np.float64)).astype(ml_dtypes.bfloat16)
    return hi, lo


def dot(a, b):
    return lax.dot_general(a, b, (((1,), (0,)), ((), ())), preferred_element_type=F32)


def split(v):
    hi = v.astype(BF16)
    return hi, (v - hi.astype(F32)).astype(BF16)


def add_halves(both):
    return both[:, :BS] + both[:, BS:]


def left_times(left, v):
    hi, lo = split(v)
    top = jnp.concatenate([hi, lo], axis=1)
    low = jnp.concatenate([hi, jnp.zeros_like(lo)], axis=1)
    return add_halves(dot(left, jnp.concatenate([top, low], axis=0)))


def pack_kernel(pos, g, *outs):
    c, x = pos[1], pos[2]
    for s in range(NX):
        for half, core in enumerate((c, 1 - c)):
            base = NZ * NC * ((x + s) % 4) + core
            for m in range(4):
                for w in range(4):
                    start = pl.multiple_of((base + 2 * (4 * w + m)) * BS, BS)
                    outs[s][half, 4 * m + w] = g[0, :, pl.ds(start, BS)]


def give_kernel(*refs):
    for s in range(NX):
        refs[NX][s] = refs[s][1]


def by_place(pos, rows, body):
    for p in range(4):
        for c in range(2):
            mine = [v.at[0] for v in rows[:NX]]
            other = [rows[NX].at[s] for s in range(NX)]
            pair = (mine, other) if c == 0 else (other, mine)
            pl.when((pos[0] == p) & (pos[1] == c))(functools.partial(body, p, *pair))


def exchange_kernel(pos, *refs):
    a, b = refs[-2:]

    def body(p, los, his):
        for r in range(NX):
            lo, hi = los[r], his[r]
            if p in (0, 3):
                s = slice(0, 4) if p == 0 else slice(12, 16)
                a[r, :, 0:48] = lo[s]
                a[r, :, 48:96] = hi[s]
                continue
            for k in range(3):
                if p == 1:
                    a[r, :, 32 * k : 32 * k + 32] = lo[4 * k + 4 : 4 * k + 8, 0:32]
                else:
                    a[r, :, 32 * k : 32 * k + 32] = hi[4 * k : 4 * k + 4, 16:48]
            if p == 1:
                b[r, :, 0:16] = lo[0:8, 32:48]
                b[r, :, 16:64] = hi[0:8]
            else:
                b[r, :, 0:48] = lo[8:16]
                b[r, :, 48:64] = hi[8:16, 0:16]

    by_place(pos, refs[:-2], body)


def assemble(pos, rows, a, b, whole):
    def place(p, k, lo, hi, r):
        m = k + (k >= p)
        d = slice(4 * k, 4 * k + 4)
        s = slice(4 * m, 4 * m + 4)
        third = slice(32 * k, 32 * k + 32)
        if p == 0:
            whole[r, d, 0:48] = lo[s]
            whole[r, d, 48:96] = hi[s]
            whole[r, d, 96:128] = a[r, :, third]
        elif p == 3:
            whole[r, d, 0:32] = a[r, :, third]
            whole[r, d, 32:80] = lo[s]
            whole[r, d, 80:128] = hi[s]
        elif p == 1 and m == 0:
            whole[r, d, 0:96] = a[r]
            whole[r, d, 96:128] = lo[s, 0:32]
        elif p == 1:
            whole[r, d, 0:16] = lo[s, 32:48]
            whole[r, d, 16:64] = hi[s]
            whole[r, d, 64:128] = b[r, 4 * (m - 2) : 4 * (m - 2) + 4]
        elif m == 3:
            whole[r, d, 0:32] = hi[s, 16:48]
            whole[r, d, 32:128] = a[r]
        else:
            whole[r, d, 0:64] = b[r, s]
            whole[r, d, 64:112] = lo[s]
            whole[r, d, 112:128] = hi[s, 0:16]

    def body(p, los, his):
        for k in range(3):
            for r in range(NX):
                place(p, k, los[r], his[r], r)

    by_place(pos, rows, body)


def exponent(size):
    return jnp.clip(jnp.floor(jnp.log2(jnp.maximum(size, F32(1e-30)))) + 1.0, -100.0, 200.0)


def forward_kernel(pos, cut, *refs):
    a, b, left, wide, out, x, exps = refs[NX + 1 :]
    assemble(pos, refs[: NX + 1], a, b, x)
    p = pos[0]
    freq = lax.broadcasted_iota(jnp.int32, (BS, BS), 0) + lax.broadcasted_iota(jnp.int32, (BS, BS), 1)
    row = lax.broadcasted_iota(jnp.int32, (TAIL, BS), 0)
    exps[...] = jnp.zeros_like(exps)
    for w in range(4):
        out[4 * w + p, 0:BS] = jnp.zeros((BS, BS), jnp.int16)

    def step(w, square):
        for k in range(3):
            m = k + (k >= p).astype(jnp.int32)
            blk = p - (p > m).astype(jnp.int32)
            total = jnp.zeros((BS, BS), F32)
            for r in range(NX):
                coef = left_times(left[...], add_halves(dot(x[r, 4 * k + w], wide[...])))
                total += jnp.where(freq <= cut[4 * w + m, 4 * blk + (pos[2] + 4 - r) % 4], coef, 0.0)
            e = exponent(jnp.max(jnp.abs(total), axis=0, keepdims=True))
            code = jnp.clip(jnp.floor(total * jnp.exp2(15.0 - e) + 0.5), -32767.0, 32767.0)
            out[4 * w + m, 0:BS] = code.astype(jnp.int32).astype(jnp.int16)
            exps[pl.ds(4 * w + m, 1), :] = e
            square += jnp.sum(total * total, axis=0, keepdims=True)
        return square

    square = jnp.zeros((1, BS), F32)
    for w in range(4):
        square = step(w, square)
    e = exponent(square)
    scaled = jnp.minimum(square, F32(3e38)) * jnp.exp2(-0.5 * e) * jnp.exp2(-0.5 * e) * 16384.0
    d1 = jnp.floor(scaled)
    d2 = jnp.floor((scaled - d1) * 16384.0)
    e = jnp.where(square > F32(3e38), 200.0, e)
    tail = jnp.where(row == 1, e, jnp.where(row == 2, d1, jnp.where(row == 3, d2, 0.0)))
    for s in range(NZ):
        mix = jnp.where(row == 0, exps[s : s + 1, :], tail)
        out[s, BS : BS + TAIL] = mix.astype(jnp.int32).astype(jnp.int16)


def compact_kernel(pos, z, out, norm):
    p = pos[0]
    row = lax.broadcasted_iota(jnp.int32, (TAIL, BS), 0)
    tail = jnp.zeros((TAIL, BS), F32)
    for g in range(4):
        for blk in range(3):
            src = 4 * g + blk + (p <= blk).astype(jnp.int32)
            n = 3 * g + blk
            out[BS * n : BS * n + BS] = z[src, 0:BS]
            e = z[src, BS : BS + TAIL].astype(jnp.int32).astype(F32)[0:1]
            tail = jnp.where(row == n, e, tail)
    out[BS * BPO : BS * BPO + TAIL] = tail.astype(jnp.int32).astype(jnp.int16)
    total = jnp.zeros((1, BS), F32)
    for s in range(NZ):
        t = z[s, BS : BS + TAIL].astype(jnp.int32).astype(F32)
        part = t[2:3] * F32(1.0 / 16384.0) + t[3:4] * F32(1.0 / 16384.0**2)
        total += part * jnp.exp2(0.5 * t[1:2]) * jnp.exp2(0.5 * t[1:2])
    norm[...] = jnp.broadcast_to(total[None], norm.shape)


def update_kernel(code, tail, norm, clip, params, mom, left, full, new_p, new_m):
    i = pl.program_id(0)
    total = jnp.sum(jnp.sum(norm[...], axis=0), axis=1, keepdims=True)
    factor = jnp.minimum(F32(1.0), clip[0] * F32(math.sqrt(D * FF)) / (jnp.sqrt(total) + F32(EPSILON)))
    row = lax.broadcasted_iota(jnp.int32, (TAIL, BS), 0)
    exps = tail[...].astype(jnp.int32).astype(F32)
    for n in range(3):
        e = jnp.sum(jnp.where(row == 3 * i + n, exps, 0.0), axis=0, keepdims=True)
        d = slice(BS * n, BS * n + BS)
        coef = code[d].astype(jnp.int32).astype(F32) * (jnp.exp2(e - 15.0) * factor)
        right = add_halves(dot(jnp.concatenate(split(coef), axis=1), full[...]))
        upd = left_times(left[...], right)
        nm = NESTEROV * mom[d] + upd
        new_m[d] = nm
        new_p[d] = params[d] - OUTER_RATE * (upd + NESTEROV * nm)


SMEM = pl.BlockSpec(memory_space=pltpu.SMEM)
VMEM = pl.BlockSpec(memory_space=pltpu.VMEM)
BIG = pltpu.CompilerParams(vmem_limit_bytes=40 * 1024 * 1024)


def call(kernel, out_shape, inputs, name, scratch=()):
    return pl.pallas_call(
        kernel,
        out_shape=out_shape,
        in_specs=[SMEM if i.dtype == jnp.int32 else VMEM for i in inputs],
        out_specs=jax.tree.map(lambda _: VMEM, out_shape),
        scratch_shapes=scratch,
        compiler_params=BIG,
        name=name,
    )(*inputs)


def per_device(pseudo_grads, outer_params, momentum, clip_level, block_picks, cutoffs):
    z = lax.axis_index("z")
    pos = jnp.stack([z % 4, lax.axis_index("c"), lax.axis_index("x")]).astype(jnp.int32)
    hi, lo = table_parts()
    fwd_wide = jnp.asarray(np.concatenate([hi.T, lo.T], axis=1))
    left = jnp.asarray(np.concatenate([hi, lo], axis=1))
    inv_full = jnp.asarray(np.block([[hi, lo], [hi, np.zeros_like(lo)]]))
    rows = pseudo_grads.shape[1]
    swap = [(NY * i + j, NX * j + i) for i in range(NX) for j in range(NY)]
    shape = jax.ShapeDtypeStruct

    picks, cuts = (
        lax.dynamic_index_in_dim(v[:, 0], lax.axis_index("x"), 1, keepdims=False) for v in (block_picks, cutoffs)
    )
    hit = picks[:, :, None] == jnp.arange(BPO, dtype=jnp.int32)
    cut = jnp.max(jnp.where(hit, cuts[:, :, None], -1), axis=1)
    cut = jnp.broadcast_to(cut.T.reshape(4, 1, BPO), (4, 4, BPO)).reshape(NZ, 1, BPO)
    cut = jnp.broadcast_to(jnp.pad(cut, ((0, 0), (0, 0), (0, BS - BPO))), (NZ, 16, BS))
    cut, pseudo_grads = lax.optimization_barrier((cut, pseudo_grads))
    cut = lax.all_to_all(cut, "z", 0, 0, tiled=True)[:, 0]

    packed = call(pack_kernel, [shape((NC, NZ, rows, BS), BF16)] * NX, (pos, pseudo_grads), "pack")
    spread = [packed[0]] + [
        lax.ppermute(packed[n], "x", [(i, (i + n) % NX) for i in range(NX)]) for n in range(1, NX)
    ]
    *spread, cut = lax.optimization_barrier((*spread, cut))
    give = call(give_kernel, shape((NX, NZ, rows, BS), BF16), spread, "give")
    spread.append(lax.ppermute(give, "c", [(0, 1), (1, 0)]))
    cut = lax.ppermute(cut, ("x", "y"), swap)

    a, b = call(
        exchange_kernel,
        (shape((NX, 4, 96, BS), BF16), shape((NX, 8, 64, BS), BF16)),
        (pos, *spread),
        "exchange",
    )
    pair_a, pair_b = [], []
    for g in range(0, NZ, 4):
        pair_a += [(g, g + 1), (g + 1, g), (g + 2, g + 3), (g + 3, g + 2)]
        pair_b += [(g + 1, g + 2), (g + 2, g + 1)]
    a = lax.ppermute(a, "z", pair_a)
    b = lax.ppermute(b, "z", pair_b)

    coded = call(
        forward_kernel,
        shape((NZ, BS + TAIL, BS), jnp.int16),
        (pos, cut, *spread, a, b, left, fwd_wide),
        "forward",
        [pltpu.VMEM((NX, BPO, BS, BS), BF16), pltpu.VMEM((NZ, BS), F32)],
    )
    coded = lax.all_to_all(coded, "z", 0, 0, tiled=True)
    coded, norm = call(
        compact_kernel,
        (shape((BPO * BS + TAIL, BS), jnp.int16), shape((NX * NY * NC, 1, BS), F32)),
        (pos, coded),
        "compact",
    )
    coded = lax.ppermute(coded, ("x", "y"), swap)
    norm = lax.all_to_all(norm, ("x", "y", "c"), 0, 0, tiled=True)

    tile = pl.BlockSpec((3 * BS, BS), lambda i: (i, 0))
    return pl.pallas_call(
        update_kernel,
        out_shape=(shape(outer_params.shape, F32), shape(outer_params.shape, F32)),
        grid=(4,),
        in_specs=[
            tile,
            pl.BlockSpec((TAIL, BS), lambda i: (BPO * BS // TAIL, 0)),
            VMEM,
            SMEM,
            tile,
            tile,
            VMEM,
            VMEM,
        ],
        out_specs=(tile, tile),
        compiler_params=BIG,
        name="update",
    )(coded, coded, norm, clip_level, outer_params, momentum, fwd_wide, inv_full)


def solution(mesh):
    grid = Mesh(mesh.devices.reshape(NX, NY, NZ, NC), ("x", "y", "z", "c"))
    yzc = ("y", "z", "c")
    in_specs = (P("x", yzc, None), P("x", yzc), P("x", yzc), P(), P(None, yzc, None, None), P(None, yzc, None, None))
    out_specs = (P("x", yzc), P("x", yzc))
    return jax.shard_map(per_device, mesh=grid, in_specs=in_specs, out_specs=out_specs, check_vma=False)
```

```python
import functools
import math

import jax
import jax.numpy as jnp
import ml_dtypes
import numpy as np
from jax import lax
from jax.experimental import pallas as pl
from jax.experimental.pallas import tpu as pltpu
from jax.sharding import Mesh, PartitionSpec as P

BS = 128
D = 6144
FF = 16384
OUTER_RATE = 0.7
NESTEROV = 0.9
EPSILON = 1e-06
NX, NY, NZ, NC = 4, 4, 16, 2
BPO = 12
TAIL = 16
F32 = jnp.float32
BF16 = jnp.bfloat16


def table_parts():
    u = np.arange(BS, dtype=np.float64)[:, None]
    k = np.arange(BS, dtype=np.float64)[None, :]
    c = np.cos(math.pi * (2.0 * k + 1.0) * u / (2.0 * BS)) * math.sqrt(2.0 / BS)
    c[0] *= math.sqrt(0.5)
    hi = c.astype(ml_dtypes.bfloat16)
    lo = (c - hi.astype(np.float64)).astype(ml_dtypes.bfloat16)
    return hi, lo


def dot(a, b):
    return lax.dot_general(a, b, (((1,), (0,)), ((), ())), preferred_element_type=F32)


def split(v):
    hi = v.astype(BF16)
    return hi, (v - hi.astype(F32)).astype(BF16)


def times_wide(v, wide):
    hi, lo = split(v)
    both = dot(hi, wide)
    return both[:, :BS] + both[:, BS:] + dot(lo, wide[:, :BS])


def tall_times(tall, v):
    hi, lo = split(v)
    both = dot(tall, hi)
    return both[:BS] + both[BS:] + dot(tall[:BS], lo)


def pack_kernel(pos, picks, cuts, g, *outs):
    c, x = pos[1], pos[2]
    lane = lax.broadcasted_iota(jnp.int32, (1, BS), 1)
    for grp in range(4):
        row = jnp.full((1, BS), -1, jnp.int32)
        for r in range(NX):
            for s in range(picks.shape[3]):
                at = 4 * picks[r, 0, x, s] + r - 12 * grp
                row = jnp.where(lane == at, jnp.maximum(row, cuts[r, 0, x, s]), row)
        for n in range(4):
            outs[NX][4 * grp + n] = row
    for s in range(NX):
        for half, core in enumerate((c, 1 - c)):
            base = NZ * NC * ((x + s) % 4) + core
            for m in range(4):
                for w in range(4):
                    start = pl.multiple_of((base + 2 * (4 * w + m)) * BS, BS)
                    outs[s][half, 4 * m + w] = g[0, :, pl.ds(start, BS)]


def give_kernel(*refs):
    for s in range(NX):
        refs[NX][s] = refs[s][1]


def by_place(pos, rows, body):
    for p in range(4):
        for c in range(2):
            mine = [v.at[0] for v in rows[:NX]]
            other = [rows[NX].at[s] for s in range(NX)]
            pair = (mine, other) if c == 0 else (other, mine)
            pl.when((pos[0] == p) & (pos[1] == c))(functools.partial(body, p, *pair))


def exchange_kernel(pos, *refs):
    a, b = refs[-2:]

    def body(p, los, his):
        for r in range(NX):
            lo, hi = los[r], his[r]
            if p in (0, 3):
                s = slice(0, 4) if p == 0 else slice(12, 16)
                a[r, :, 0:48] = lo[s]
                a[r, :, 48:96] = hi[s]
                continue
            for k in range(3):
                if p == 1:
                    a[r, :, 32 * k : 32 * k + 32] = lo[4 * k + 4 : 4 * k + 8, 0:32]
                else:
                    a[r, :, 32 * k : 32 * k + 32] = hi[4 * k : 4 * k + 4, 16:48]
            if p == 1:
                b[r, :, 0:16] = lo[0:8, 32:48]
                b[r, :, 16:64] = hi[0:8]
            else:
                b[r, :, 0:48] = lo[8:16]
                b[r, :, 48:64] = hi[8:16, 0:16]

    by_place(pos, refs[:-2], body)


def assemble(pos, rows, a, b, whole):
    def place(p, k, lo, hi, r):
        m = k + (k >= p)
        d = slice(4 * k, 4 * k + 4)
        s = slice(4 * m, 4 * m + 4)
        third = slice(32 * k, 32 * k + 32)
        if p == 0:
            whole[r, d, 0:48] = lo[s]
            whole[r, d, 48:96] = hi[s]
            whole[r, d, 96:128] = a[r, :, third]
        elif p == 3:
            whole[r, d, 0:32] = a[r, :, third]
            whole[r, d, 32:80] = lo[s]
            whole[r, d, 80:128] = hi[s]
        elif p == 1 and m == 0:
            whole[r, d, 0:96] = a[r]
            whole[r, d, 96:128] = lo[s, 0:32]
        elif p == 1:
            whole[r, d, 0:16] = lo[s, 32:48]
            whole[r, d, 16:64] = hi[s]
            whole[r, d, 64:128] = b[r, 4 * (m - 2) : 4 * (m - 2) + 4]
        elif m == 3:
            whole[r, d, 0:32] = hi[s, 16:48]
            whole[r, d, 32:128] = a[r]
        else:
            whole[r, d, 0:64] = b[r, s]
            whole[r, d, 64:112] = lo[s]
            whole[r, d, 112:128] = hi[s, 0:16]

    def body(p, los, his):
        for k in range(3):
            for r in range(NX):
                place(p, k, los[r], his[r], r)

    by_place(pos, rows, body)


def exponent(size):
    return jnp.clip(jnp.floor(jnp.log2(jnp.maximum(size, F32(1e-30)))) + 1.0, -100.0, 200.0)


def forward_kernel(pos, cut, *refs):
    a, b, left, wide, out, x, exps = refs[NX + 1 :]
    assemble(pos, refs[: NX + 1], a, b, x)
    p = pos[0]
    freq = lax.broadcasted_iota(jnp.int32, (BS, BS), 0) + lax.broadcasted_iota(jnp.int32, (BS, BS), 1)
    row = lax.broadcasted_iota(jnp.int32, (TAIL, BS), 0)
    exps[...] = jnp.zeros_like(exps)
    for w in range(4):
        out[4 * w + p, 0:BS] = jnp.zeros((BS, BS), jnp.int16)

    def step(w, square):
        for k in range(3):
            m = k + (k >= p).astype(jnp.int32)
            blk = p - (p > m).astype(jnp.int32)
            total = jnp.zeros((BS, BS), F32)
            for r in range(NX):
                both = dot(x[r, 4 * k + w], wide[...])
                hi, lo = split(both[:, :BS] + both[:, BS:])
                pairs = jnp.concatenate(
                    [
                        jnp.concatenate([hi, lo], axis=1),
                        jnp.concatenate([hi, jnp.zeros_like(lo)], axis=1),
                    ],
                    axis=0,
                )
                both = dot(left[...], pairs)
                coef = both[:, :BS] + both[:, BS:]
                total += jnp.where(freq <= cut[4 * w + m, 4 * blk + (pos[2] + 4 - r) % 4], coef, 0.0)
            e = exponent(jnp.max(jnp.abs(total), axis=0, keepdims=True))
            code = jnp.clip(jnp.floor(total * jnp.exp2(15.0 - e) + 0.5), -32767.0, 32767.0)
            out[4 * w + m, 0:BS] = code.astype(jnp.int32).astype(jnp.int16)
            exps[pl.ds(4 * w + m, 1), :] = e
            square += jnp.sum(total * total, axis=0, keepdims=True)
        return square

    square = jnp.zeros((1, BS), F32)
    for w in range(4):
        square = step(w, square)
    e = exponent(square)
    scaled = jnp.minimum(square, F32(3e38)) * jnp.exp2(-0.5 * e) * jnp.exp2(-0.5 * e) * 16384.0
    d1 = jnp.floor(scaled)
    d2 = jnp.floor((scaled - d1) * 16384.0)
    e = jnp.where(square > F32(3e38), 200.0, e)
    tail = jnp.where(row == 1, e, jnp.where(row == 2, d1, jnp.where(row == 3, d2, 0.0)))
    for s in range(NZ):
        mix = jnp.where(row == 0, exps[s : s + 1, :], tail)
        out[s, BS : BS + TAIL] = mix.astype(jnp.int32).astype(jnp.int16)


def compact_kernel(pos, z, out, norm):
    p = pos[0]
    row = lax.broadcasted_iota(jnp.int32, (TAIL, BS), 0)
    tail = jnp.zeros((TAIL, BS), F32)
    for g in range(4):
        for blk in range(3):
            src = 4 * g + blk + (p <= blk).astype(jnp.int32)
            n = 3 * g + blk
            out[BS * n : BS * n + BS] = z[src, 0:BS]
            e = z[src, BS : BS + TAIL].astype(jnp.int32).astype(F32)[0:1]
            tail = jnp.where(row == n, e, tail)
    out[BS * BPO : BS * BPO + TAIL] = tail.astype(jnp.int32).astype(jnp.int16)
    total = jnp.zeros((1, BS), F32)
    for s in range(NZ):
        t = z[s, BS : BS + TAIL].astype(jnp.int32).astype(F32)
        part = t[2:3] * F32(1.0 / 16384.0) + t[3:4] * F32(1.0 / 16384.0**2)
        total += part * jnp.exp2(0.5 * t[1:2]) * jnp.exp2(0.5 * t[1:2])
    norm[...] = jnp.broadcast_to(total[None], norm.shape)


def update_kernel(code, tail, norm, clip, params, mom, tall, wide, new_p, new_m):
    i = pl.program_id(0)
    total = jnp.sum(jnp.sum(norm[...], axis=0), axis=1, keepdims=True)
    factor = jnp.minimum(F32(1.0), clip[0] * F32(math.sqrt(D * FF)) / (jnp.sqrt(total) + F32(EPSILON)))
    row = lax.broadcasted_iota(jnp.int32, (TAIL, BS), 0)
    exps = tail[...].astype(jnp.int32).astype(F32)
    for n in range(3):
        e = jnp.sum(jnp.where(row == 3 * i + n, exps, 0.0), axis=0, keepdims=True)
        d = slice(BS * n, BS * n + BS)
        coef = code[d].astype(jnp.int32).astype(F32) * (jnp.exp2(e - 15.0) * factor)
        upd = tall_times(tall[...], times_wide(coef, wide[...]))
        nm = NESTEROV * mom[d] + upd
        new_m[d] = nm
        new_p[d] = params[d] - OUTER_RATE * (upd + NESTEROV * nm)


SMEM = pl.BlockSpec(memory_space=pltpu.SMEM)
VMEM = pl.BlockSpec(memory_space=pltpu.VMEM)
BIG = pltpu.CompilerParams(vmem_limit_bytes=40 * 1024 * 1024)


def call(kernel, out_shape, inputs, name, scratch=()):
    return pl.pallas_call(
        kernel,
        out_shape=out_shape,
        in_specs=[SMEM if i.dtype == jnp.int32 else VMEM for i in inputs],
        out_specs=jax.tree.map(lambda _: VMEM, out_shape),
        scratch_shapes=scratch,
        compiler_params=BIG,
        name=name,
    )(*inputs)


def per_device(pseudo_grads, outer_params, momentum, clip_level, block_picks, cutoffs):
    z = lax.axis_index("z")
    pos = jnp.stack([z % 4, lax.axis_index("c"), lax.axis_index("x")]).astype(jnp.int32)
    hi, lo = table_parts()
    fwd_wide = jnp.asarray(np.concatenate([hi.T, lo.T], axis=1))
    inv_wide = jnp.asarray(np.concatenate([hi, lo], axis=1))
    inv_tall = jnp.asarray(np.concatenate([hi.T, lo.T], axis=0))
    rows = pseudo_grads.shape[1]
    swap = [(NY * i + j, NX * j + i) for i in range(NX) for j in range(NY)]
    shape = jax.ShapeDtypeStruct

    *packed, cut = call(
        pack_kernel,
        [shape((NC, NZ, rows, BS), BF16)] * NX + [shape((NZ, 1, BS), jnp.int32)],
        (pos, block_picks, cutoffs, pseudo_grads),
        "pack",
    )
    cut = lax.all_to_all(cut, "z", 0, 0, tiled=True)[:, 0]
    spread = [packed[0]] + [
        lax.ppermute(packed[n], "x", [(i, (i + n) % NX) for i in range(NX)]) for n in range(1, NX)
    ]
    *spread, cut = lax.optimization_barrier((*spread, cut))
    give = call(give_kernel, shape((NX, NZ, rows, BS), BF16), spread, "give")
    spread.append(lax.ppermute(give, "c", [(0, 1), (1, 0)]))
    cut = lax.ppermute(cut, ("x", "y"), swap)

    a, b = call(
        exchange_kernel,
        (shape((NX, 4, 96, BS), BF16), shape((NX, 8, 64, BS), BF16)),
        (pos, *spread),
        "exchange",
    )
    pair_a, pair_b = [], []
    for g in range(0, NZ, 4):
        pair_a += [(g, g + 1), (g + 1, g), (g + 2, g + 3), (g + 3, g + 2)]
        pair_b += [(g + 1, g + 2), (g + 2, g + 1)]
    a = lax.ppermute(a, "z", pair_a)
    b = lax.ppermute(b, "z", pair_b)

    coded = call(
        forward_kernel,
        shape((NZ, BS + TAIL, BS), jnp.int16),
        (pos, cut, *spread, a, b, inv_wide, fwd_wide),
        "forward",
        [pltpu.VMEM((NX, BPO, BS, BS), BF16), pltpu.VMEM((NZ, BS), F32)],
    )
    coded = lax.all_to_all(coded, "z", 0, 0, tiled=True)
    coded, norm = call(
        compact_kernel,
        (shape((BPO * BS + TAIL, BS), jnp.int16), shape((NX * NY * NC, 1, BS), F32)),
        (pos, coded),
        "compact",
    )
    coded = lax.ppermute(coded, ("x", "y"), swap)
    norm = lax.all_to_all(norm, ("x", "y", "c"), 0, 0, tiled=True)

    tile = pl.BlockSpec((3 * BS, BS), lambda i: (i, 0))
    return pl.pallas_call(
        update_kernel,
        out_shape=(shape(outer_params.shape, F32), shape(outer_params.shape, F32)),
        grid=(4,),
        in_specs=[
            tile,
            pl.BlockSpec((TAIL, BS), lambda i: (BPO * BS // TAIL, 0)),
            VMEM,
            SMEM,
            tile,
            tile,
            VMEM,
            VMEM,
        ],
        out_specs=(tile, tile),
        compiler_params=BIG,
        name="update",
    )(coded, coded, norm, clip_level, outer_params, momentum, inv_tall, inv_wide)


def solution(mesh):
    grid = Mesh(mesh.devices.reshape(NX, NY, NZ, NC), ("x", "y", "z", "c"))
    yzc = ("y", "z", "c")
    in_specs = (P("x", yzc, None), P("x", yzc), P("x", yzc), P(), P(None, yzc, None, None), P(None, yzc, None, None))
    out_specs = (P("x", yzc), P("x", yzc))
    return jax.shard_map(per_device, mesh=grid, in_specs=in_specs, out_specs=out_specs, check_vma=False)
```

```python
import functools
import math

import jax
import jax.numpy as jnp
import ml_dtypes
import numpy as np
from jax import lax
from jax.experimental import pallas as pl
from jax.experimental.pallas import tpu as pltpu
from jax.sharding import Mesh, PartitionSpec as P

BS = 128
D = 6144
FF = 16384
OUTER_RATE = 0.7
NESTEROV = 0.9
EPSILON = 1e-06
NX, NY, NZ, NC = 4, 4, 16, 2
BPO = 12
TAIL = 16
F32 = jnp.float32
BF16 = jnp.bfloat16


def table_parts():
    u = np.arange(BS, dtype=np.float64)[:, None]
    k = np.arange(BS, dtype=np.float64)[None, :]
    c = np.cos(math.pi * (2.0 * k + 1.0) * u / (2.0 * BS)) * math.sqrt(2.0 / BS)
    c[0] *= math.sqrt(0.5)
    hi = c.astype(ml_dtypes.bfloat16)
    lo = (c - hi.astype(np.float64)).astype(ml_dtypes.bfloat16)
    return hi, lo


def dot(a, b):
    return lax.dot_general(a, b, (((1,), (0,)), ((), ())), preferred_element_type=F32)


def split(v):
    hi = v.astype(BF16)
    return hi, (v - hi.astype(F32)).astype(BF16)


def add_halves(both):
    return both[:, :BS] + both[:, BS:]


def left_times(left, v):
    hi, lo = split(v)
    top = jnp.concatenate([hi, lo], axis=1)
    low = jnp.concatenate([hi, jnp.zeros_like(lo)], axis=1)
    return add_halves(dot(left, jnp.concatenate([top, low], axis=0)))


def pack_kernel(pos, picks, cuts, g, *outs):
    c, x = pos[1], pos[2]
    lane = lax.broadcasted_iota(jnp.int32, (1, BS), 1)
    for grp in range(4):
        row = jnp.full((1, BS), -1, jnp.int32)
        for r in range(NX):
            for s in range(picks.shape[3]):
                at = 4 * picks[r, 0, x, s] + r - 12 * grp
                row = jnp.where(lane == at, jnp.maximum(row, cuts[r, 0, x, s]), row)
        for n in range(4):
            outs[NX][4 * grp + n] = row
    for s in range(NX):
        for half, core in enumerate((c, 1 - c)):
            base = NZ * NC * ((x + s) % 4) + core
            for m in range(4):
                for w in range(4):
                    start = pl.multiple_of((base + 2 * (4 * w + m)) * BS, BS)
                    outs[s][half, 4 * m + w] = g[0, :, pl.ds(start, BS)]


def give_kernel(*refs):
    for s in range(NX):
        refs[NX][s] = refs[s][1]


def by_place(pos, rows, body):
    for p in range(4):
        for c in range(2):
            mine = [v.at[0] for v in rows[:NX]]
            other = [rows[NX].at[s] for s in range(NX)]
            pair = (mine, other) if c == 0 else (other, mine)
            pl.when((pos[0] == p) & (pos[1] == c))(functools.partial(body, p, *pair))


def exchange_kernel(pos, *refs):
    a, b = refs[-2:]

    def body(p, los, his):
        for r in range(NX):
            lo, hi = los[r], his[r]
            if p in (0, 3):
                s = slice(0, 4) if p == 0 else slice(12, 16)
                a[r, :, 0:48] = lo[s]
                a[r, :, 48:96] = hi[s]
                continue
            for k in range(3):
                if p == 1:
                    a[r, :, 32 * k : 32 * k + 32] = lo[4 * k + 4 : 4 * k + 8, 0:32]
                else:
                    a[r, :, 32 * k : 32 * k + 32] = hi[4 * k : 4 * k + 4, 16:48]
            if p == 1:
                b[r, :, 0:16] = lo[0:8, 32:48]
                b[r, :, 16:64] = hi[0:8]
            else:
                b[r, :, 0:48] = lo[8:16]
                b[r, :, 48:64] = hi[8:16, 0:16]

    by_place(pos, refs[:-2], body)


def assemble(pos, rows, a, b, whole):
    def place(p, k, lo, hi, r):
        m = k + (k >= p)
        d = slice(4 * k, 4 * k + 4)
        s = slice(4 * m, 4 * m + 4)
        third = slice(32 * k, 32 * k + 32)
        if p == 0:
            whole[r, d, 0:48] = lo[s]
            whole[r, d, 48:96] = hi[s]
            whole[r, d, 96:128] = a[r, :, third]
        elif p == 3:
            whole[r, d, 0:32] = a[r, :, third]
            whole[r, d, 32:80] = lo[s]
            whole[r, d, 80:128] = hi[s]
        elif p == 1 and m == 0:
            whole[r, d, 0:96] = a[r]
            whole[r, d, 96:128] = lo[s, 0:32]
        elif p == 1:
            whole[r, d, 0:16] = lo[s, 32:48]
            whole[r, d, 16:64] = hi[s]
            whole[r, d, 64:128] = b[r, 4 * (m - 2) : 4 * (m - 2) + 4]
        elif m == 3:
            whole[r, d, 0:32] = hi[s, 16:48]
            whole[r, d, 32:128] = a[r]
        else:
            whole[r, d, 0:64] = b[r, s]
            whole[r, d, 64:112] = lo[s]
            whole[r, d, 112:128] = hi[s, 0:16]

    def body(p, los, his):
        for k in range(3):
            for r in range(NX):
                place(p, k, los[r], his[r], r)

    by_place(pos, rows, body)


def exponent(size):
    return jnp.clip(jnp.floor(jnp.log2(jnp.maximum(size, F32(1e-30)))) + 1.0, -100.0, 200.0)


def forward_kernel(pos, cut, *refs):
    a, b, left, wide, out, x, exps = refs[NX + 1 :]
    assemble(pos, refs[: NX + 1], a, b, x)
    p = pos[0]
    freq = lax.broadcasted_iota(jnp.int32, (BS, BS), 0) + lax.broadcasted_iota(jnp.int32, (BS, BS), 1)
    row = lax.broadcasted_iota(jnp.int32, (TAIL, BS), 0)
    exps[...] = jnp.zeros_like(exps)
    for w in range(4):
        out[4 * w + p, 0:BS] = jnp.zeros((BS, BS), jnp.int16)

    def step(w, square):
        for k in range(3):
            m = k + (k >= p).astype(jnp.int32)
            blk = p - (p > m).astype(jnp.int32)
            total = jnp.zeros((BS, BS), F32)
            for r in range(NX):
                coef = left_times(left[...], add_halves(dot(x[r, 4 * k + w], wide[...])))
                total += jnp.where(freq <= cut[4 * w + m, 4 * blk + (pos[2] + 4 - r) % 4], coef, 0.0)
            e = exponent(jnp.max(jnp.abs(total), axis=0, keepdims=True))
            code = jnp.clip(jnp.floor(total * jnp.exp2(15.0 - e) + 0.5), -32767.0, 32767.0)
            out[4 * w + m, 0:BS] = code.astype(jnp.int32).astype(jnp.int16)
            exps[pl.ds(4 * w + m, 1), :] = e
            square += jnp.sum(total * total, axis=0, keepdims=True)
        return square

    square = jnp.zeros((1, BS), F32)
    for w in range(4):
        square = step(w, square)
    e = exponent(square)
    scaled = jnp.minimum(square, F32(3e38)) * jnp.exp2(-0.5 * e) * jnp.exp2(-0.5 * e) * 16384.0
    d1 = jnp.floor(scaled)
    d2 = jnp.floor((scaled - d1) * 16384.0)
    e = jnp.where(square > F32(3e38), 200.0, e)
    tail = jnp.where(row == 1, e, jnp.where(row == 2, d1, jnp.where(row == 3, d2, 0.0)))
    for s in range(NZ):
        mix = jnp.where(row == 0, exps[s : s + 1, :], tail)
        out[s, BS : BS + TAIL] = mix.astype(jnp.int32).astype(jnp.int16)


def compact_kernel(pos, z, out, norm):
    p = pos[0]
    row = lax.broadcasted_iota(jnp.int32, (TAIL, BS), 0)
    tail = jnp.zeros((TAIL, BS), F32)
    for g in range(4):
        for blk in range(3):
            src = 4 * g + blk + (p <= blk).astype(jnp.int32)
            n = 3 * g + blk
            out[BS * n : BS * n + BS] = z[src, 0:BS]
            e = z[src, BS : BS + TAIL].astype(jnp.int32).astype(F32)[0:1]
            tail = jnp.where(row == n, e, tail)
    out[BS * BPO : BS * BPO + TAIL] = tail.astype(jnp.int32).astype(jnp.int16)
    total = jnp.zeros((1, BS), F32)
    for s in range(NZ):
        t = z[s, BS : BS + TAIL].astype(jnp.int32).astype(F32)
        part = t[2:3] * F32(1.0 / 16384.0) + t[3:4] * F32(1.0 / 16384.0**2)
        total += part * jnp.exp2(0.5 * t[1:2]) * jnp.exp2(0.5 * t[1:2])
    norm[...] = jnp.broadcast_to(total[None], norm.shape)


def update_kernel(code, tail, norm, clip, params, mom, left, full, new_p, new_m):
    i = pl.program_id(0)
    total = jnp.sum(jnp.sum(norm[...], axis=0), axis=1, keepdims=True)
    factor = jnp.minimum(F32(1.0), clip[0] * F32(math.sqrt(D * FF)) / (jnp.sqrt(total) + F32(EPSILON)))
    row = lax.broadcasted_iota(jnp.int32, (TAIL, BS), 0)
    exps = tail[...].astype(jnp.int32).astype(F32)
    for n in range(3):
        e = jnp.sum(jnp.where(row == 3 * i + n, exps, 0.0), axis=0, keepdims=True)
        d = slice(BS * n, BS * n + BS)
        coef = code[d].astype(jnp.int32).astype(F32) * (jnp.exp2(e - 15.0) * factor)
        right = add_halves(dot(jnp.concatenate(split(coef), axis=1), full[...]))
        upd = left_times(left[...], right)
        nm = NESTEROV * mom[d] + upd
        new_m[d] = nm
        new_p[d] = params[d] - OUTER_RATE * (upd + NESTEROV * nm)


SMEM = pl.BlockSpec(memory_space=pltpu.SMEM)
VMEM = pl.BlockSpec(memory_space=pltpu.VMEM)
BIG = pltpu.CompilerParams(vmem_limit_bytes=40 * 1024 * 1024)


def call(kernel, out_shape, inputs, name, scratch=()):
    return pl.pallas_call(
        kernel,
        out_shape=out_shape,
        in_specs=[SMEM if i.dtype == jnp.int32 else VMEM for i in inputs],
        out_specs=jax.tree.map(lambda _: VMEM, out_shape),
        scratch_shapes=scratch,
        compiler_params=BIG,
        name=name,
    )(*inputs)


def per_device(pseudo_grads, outer_params, momentum, clip_level, block_picks, cutoffs):
    z = lax.axis_index("z")
    pos = jnp.stack([z % 4, lax.axis_index("c"), lax.axis_index("x")]).astype(jnp.int32)
    hi, lo = table_parts()
    fwd_wide = jnp.asarray(np.concatenate([hi.T, lo.T], axis=1))
    left = jnp.asarray(np.concatenate([hi, lo], axis=1))
    inv_full = jnp.asarray(np.block([[hi, lo], [hi, np.zeros_like(lo)]]))
    rows = pseudo_grads.shape[1]
    swap = [(NY * i + j, NX * j + i) for i in range(NX) for j in range(NY)]
    shape = jax.ShapeDtypeStruct

    *packed, cut = call(
        pack_kernel,
        [shape((NC, NZ, rows, BS), BF16)] * NX + [shape((NZ, 1, BS), jnp.int32)],
        (pos, block_picks, cutoffs, pseudo_grads),
        "pack",
    )
    cut = lax.all_to_all(cut, "z", 0, 0, tiled=True)[:, 0]
    spread = [packed[0]] + [
        lax.ppermute(packed[n], "x", [(i, (i + n) % NX) for i in range(NX)]) for n in range(1, NX)
    ]
    *spread, cut = lax.optimization_barrier((*spread, cut))
    give = call(give_kernel, shape((NX, NZ, rows, BS), BF16), spread, "give")
    spread.append(lax.ppermute(give, "c", [(0, 1), (1, 0)]))
    cut = lax.ppermute(cut, ("x", "y"), swap)

    a, b = call(
        exchange_kernel,
        (shape((NX, 4, 96, BS), BF16), shape((NX, 8, 64, BS), BF16)),
        (pos, *spread),
        "exchange",
    )
    pair_a, pair_b = [], []
    for g in range(0, NZ, 4):
        pair_a += [(g, g + 1), (g + 1, g), (g + 2, g + 3), (g + 3, g + 2)]
        pair_b += [(g + 1, g + 2), (g + 2, g + 1)]
    a = lax.ppermute(a, "z", pair_a)
    b = lax.ppermute(b, "z", pair_b)

    coded = call(
        forward_kernel,
        shape((NZ, BS + TAIL, BS), jnp.int16),
        (pos, cut, *spread, a, b, left, fwd_wide),
        "forward",
        [pltpu.VMEM((NX, BPO, BS, BS), BF16), pltpu.VMEM((NZ, BS), F32)],
    )
    coded = lax.all_to_all(coded, "z", 0, 0, tiled=True)
    coded, norm = call(
        compact_kernel,
        (shape((BPO * BS + TAIL, BS), jnp.int16), shape((NX * NY * NC, 1, BS), F32)),
        (pos, coded),
        "compact",
    )
    coded = lax.ppermute(coded, ("x", "y"), swap)
    norm = lax.all_to_all(norm, ("x", "y", "c"), 0, 0, tiled=True)

    tile = pl.BlockSpec((3 * BS, BS), lambda i: (i, 0))
    return pl.pallas_call(
        update_kernel,
        out_shape=(shape(outer_params.shape, F32), shape(outer_params.shape, F32)),
        grid=(4,),
        in_specs=[
            tile,
            pl.BlockSpec((TAIL, BS), lambda i: (BPO * BS // TAIL, 0)),
            VMEM,
            SMEM,
            tile,
            tile,
            VMEM,
            VMEM,
        ],
        out_specs=(tile, tile),
        compiler_params=BIG,
        name="update",
    )(coded, coded, norm, clip_level, outer_params, momentum, fwd_wide, inv_full)


def solution(mesh):
    grid = Mesh(mesh.devices.reshape(NX, NY, NZ, NC), ("x", "y", "z", "c"))
    yzc = ("y", "z", "c")
    in_specs = (P("x", yzc, None), P("x", yzc), P("x", yzc), P(), P(None, yzc, None, None), P(None, yzc, None, None))
    out_specs = (P("x", yzc), P("x", yzc))
    return jax.shard_map(per_device, mesh=grid, in_specs=in_specs, out_specs=out_specs, check_vma=False)
```
